32 devices in a mesh: grp: 2 (over y), seq: 8 (over z, x), lat: 2 (over core).
Axes of the slice: x: 2, y: 2, z: 4, core: 2. Of those that a mesh axis runs over, the one named last changes fastest.
Arguments:
- codes_idx: int32 [2048, 32], P(('grp', 'seq')), parts along dimension 0, may hold values from 0 to 65535, as said below
- codes_val: bfloat16 [2048, 32], P(('grp', 'seq')), parts along dimension 0, may hold values from 0.25 to 4
- decoder: bfloat16 [16, 16384, 2048], P(('seq', 'lat')), may hold values from -1 to 1
- decoder_offset_bias: bfloat16 [8192], P(('seq', 'lat')), may hold values from -3 to 3
- norm_gain: bfloat16 [8192], P(('seq', 'lat')), may hold values from 0.25 to 1.75
- w_query: bfloat16 [8192, 1024], P(('seq', 'lat')), may hold values from -0.09375 to 0.09375
- w_key: bfloat16 [8192, 128], P(('seq', 'lat')), may hold values from -0.09375 to 0.09375
- orig_queries: bfloat16 [8, 2048, 128], P('lat', ('grp', 'seq')), parts along dimension 1, may hold values from -40 to 40
- orig_keys: bfloat16 [2048, 128], P(('grp', 'seq')), parts along dimension 0, may hold values from -2.8 to 2.8
- mask_layout: int32 [16, 3], P('grp'), parts along dimension 0, may hold values from 0 to 1, as said below
Outputs:
- grad_vals: float32 [2048, 32], P(('grp', 'seq')), parts along dimension 0
The draws below stay inside these ranges and needn't reach their ends.
There are 2 independent parts, one for each index of `grp`. The reference program is written for one: setup_inputs(seed, part) draws one part's arguments, and reference() takes and returns one part's arrays. A program takes and returns all parts, laid end to end along the dimension named above; an argument that names none is the same for every part. Nothing has to cross between parts.
Inputs may be any that keep to these rules, and one draw needn't show every extreme that they name: `codes_idx`: the 32 latents of a token are distinct. `mask_layout`: the last column is 1 in every row.
All inputs are finite; a program needn't handle non-finite values.
Results may differ from the reference program's by a relative error of at most 0.023.
Values may be sent and summed in bfloat16 or wider, within the bound.
A program may use at most 384 MiB of HBM per device.

```python
import math
import jax
import jax.numpy as jnp
from jax import lax

D = 8192
LAT = 65536
TOPK = 32
HEAD = 128
QH = 8
BLK = 128
BAND = 2
TOK_DEV = 128
TOKENS = 1024
RANGE = 512
SUB = 64
NB = 8
FCOL = 512


def key_base(key):
    return 1.4 * jnp.clip(jax.random.normal(key, (TOKENS, HEAD), jnp.float32), -2.0, 2.0)


def layout_bits(key):
    return jax.random.randint(jax.random.fold_in(key, 3), (NB, BAND), 0, 2)


def draw_codes_idx(key, part):
    key = jax.random.fold_in(key, 11)
    stride = LAT // TOPK
    start = jax.random.randint(jax.random.fold_in(key, 1), (TOKENS, 1), 0, LAT)
    gaps = jax.random.randint(jax.random.fold_in(key, 2), (TOKENS, TOPK - 1), 1, stride + 1)
    start = start.at[0, 0].set(LAT - 1)
    gaps = gaps.at[0, 0].set(1)
    offsets = jnp.concatenate([jnp.zeros((TOKENS, 1), jnp.int32), jnp.cumsum(gaps, axis=1)], axis=1)
    values = (start + offsets) % LAT
    ranks = jax.random.randint(jax.random.fold_in(key, 4), (TOKENS, TOPK), 0, 1 << 20)
    ranks = ranks * TOPK + jnp.arange(TOPK, dtype=jnp.int32)[None, :]
    order = jnp.argsort(ranks, axis=1)
    return jnp.take_along_axis(values, order, axis=1).astype(jnp.int32)


def draw_orig_keys(key, part):
    return key_base(key).astype(jnp.bfloat16)


def draw_orig_queries(key, part):
    key = jax.random.fold_in(key, 7)
    fresh = jnp.clip(1.4 * jax.random.normal(key, (QH, TOKENS, HEAD), jnp.float32), -8.0, 8.0)
    return fresh.astype(jnp.bfloat16)


def draw_mask_layout(key, part):
    earlier = layout_bits(key)
    return jnp.concatenate([earlier, jnp.ones((NB, 1), jnp.int32)], axis=1).astype(jnp.int32)


def block_scale(stream_key, dims, cuts, low, high):
    def one(dim, parts):
        steps = jax.random.uniform(jax.random.fold_in(jax.random.fold_in(stream_key, 6), dim), (parts,), jnp.float32, low / len(cuts), high / len(cuts))
        return jnp.repeat(jnp.exp(steps), dims[dim] // parts).reshape((-1,) + (1,) * (len(dims) - dim - 1))

    loudness = one(*cuts[0])
    for cut in cuts[1:]:
        loudness = loudness * one(*cut)
    return loudness


def gaussian(own_key, dims, deviation, most, cuts=(), kind=jnp.bfloat16):
    drawn = jax.random.normal(own_key, dims, jnp.float32) * deviation
    if len(cuts) > 0:
        drawn = block_scale(own_key, dims, cuts, -0.22, 0.18) * drawn
    return jnp.clip(drawn, min=-most, max=most).astype(kind)


def setup_inputs(seed: int = 0, part: int = 0) -> dict:
    arg_keys = jax.random.split(jax.random.key(seed), 11)
    own_keys = jax.random.split(jax.random.fold_in(arg_keys[10], part), 11)
    codes_idx = draw_codes_idx(jax.random.fold_in(jax.random.fold_in(arg_keys[10], part), 71), part)
    codes_val = jnp.clip(jnp.exp(math.log(4.0) - 2.7725887 * jax.random.uniform(own_keys[1], (TOKENS, TOPK), jnp.float32) ** block_scale(own_keys[1], (TOKENS, TOPK), ((0, 8),), -0.2, 0.2)), 0.25, 4.0).astype(jnp.bfloat16)
    decoder = gaussian(arg_keys[2], (D // FCOL, LAT // 4, 4 * FCOL), TOPK ** -0.5, 1.0, ((0, 16),))
    decoder_offset_bias = gaussian(arg_keys[3], (D,), 0.5, 3.0, ((0, 16),))
    norm_gain = jnp.clip(1.0 + 0.15 * jax.random.normal(arg_keys[4], (D,), jnp.float32), 0.25, 1.75).astype(jnp.bfloat16)
    w_query = gaussian(arg_keys[5], (D, QH * HEAD), (D // 2) ** -0.5, 0.09375, ((0, 16),))
    w_key = gaussian(arg_keys[6], (D, HEAD), (D // 2) ** -0.5, 0.09375, ((0, 16),))
    orig_queries = draw_orig_queries(jax.random.fold_in(jax.random.fold_in(arg_keys[10], part), 71), part)
    orig_keys = draw_orig_keys(jax.random.fold_in(jax.random.fold_in(arg_keys[10], part), 71), part)
    mask_layout = draw_mask_layout(jax.random.fold_in(jax.random.fold_in(arg_keys[10], part), 71), part)
    return dict(codes_idx=codes_idx, codes_val=codes_val, decoder=decoder, decoder_offset_bias=decoder_offset_bias, norm_gain=norm_gain, w_query=w_query, w_key=w_key, orig_queries=orig_queries, orig_keys=orig_keys, mask_layout=mask_layout)


KL_WEIGHT = 16.0
EPSILON = 1e-05

def row_of_position():
    position = jnp.arange(TOKENS, dtype=jnp.int32)
    remaining_count = position % RANGE
    return (remaining_count // SUB * TOK_DEV + position // RANGE * SUB + remaining_count % SUB).astype(jnp.int32)

def position_of_row():
    row_ids = jnp.arange(TOKENS, dtype=jnp.int32)
    within = row_ids % TOK_DEV
    return (within // SUB * RANGE + row_ids // TOK_DEV * SUB + within % SUB).astype(jnp.int32)

def key_windows(keys_pos):
    padded = jnp.concatenate([jnp.zeros((BAND * BLK, HEAD), keys_pos.dtype), keys_pos], axis=0)
    padded = padded.reshape(NB + BAND, BLK, HEAD)
    stacked = jnp.stack([padded[shift_idx:shift_idx + NB] for shift_idx in range(BAND + 1)], axis=1)
    return stacked.reshape(NB, (BAND + 1) * BLK, HEAD)

def reference(codes_idx, codes_val, decoder, decoder_offset_bias, norm_gain, w_query, w_key, orig_queries, orig_keys, mask_layout):
    block_count = D // FCOL
    decoder = jnp.transpose(decoder.reshape(block_count, LAT // 4, 4, FCOL), (1, 2, 0, 3)).reshape(LAT, D)
    step_rows = math.gcd(TOKENS, 64)
    idx_blocks = codes_idx.reshape(TOKENS // step_rows, step_rows, TOPK)
    val_blocks = codes_val.reshape(TOKENS // step_rows, step_rows, TOPK)

    def recon_block(index_value_pair):
        decoder_weight_rows = jnp.take(decoder, index_value_pair[0], axis=0).astype(jnp.float32)
        return jnp.einsum('qt,qts->qs', index_value_pair[1].astype(jnp.float32), decoder_weight_rows)
    summed = lax.map(recon_block, (idx_blocks, val_blocks)).reshape(TOKENS, D)
    residual = (summed + decoder_offset_bias.astype(jnp.float32)[None, :]).astype(jnp.bfloat16)
    resid_f32 = residual.astype(jnp.float32)
    inv_rms = lax.rsqrt(lax.optimization_barrier(jnp.mean(resid_f32 * resid_f32, axis=1)) + EPSILON)
    gain_f32 = norm_gain.astype(jnp.float32)
    normed = (resid_f32 * inv_rms[:, None] * gain_f32[None, :]).astype(jnp.bfloat16)
    queries = jnp.dot(normed, w_query, preferred_element_type=jnp.float32).astype(jnp.bfloat16)
    queries = queries.reshape(TOKENS, QH, HEAD)
    keys = jnp.dot(normed, w_key, preferred_element_type=jnp.float32).astype(jnp.bfloat16)
    row_order = row_of_position()
    query_pos = jnp.transpose(queries[row_order], (1, 0, 2))
    keys_pos = keys[row_order]
    old_query_pos = orig_queries[:, row_order]
    old_keys_pos = orig_keys[row_order]
    win_len = (BAND + 1) * BLK
    win_slot = jnp.arange(win_len, dtype=jnp.int32) // BLK
    win_inner = jnp.arange(win_len, dtype=jnp.int32) % BLK
    query_idx = jnp.arange(BLK, dtype=jnp.int32)
    block_ids = jnp.arange(NB, dtype=jnp.int32)
    layout = mask_layout[:, win_slot] > 0
    exists = block_ids[:, None] - BAND + win_slot[None, :] >= 0
    causal = (win_slot[None, :] < BAND) | (win_inner[None, :] <= query_idx[:, None])
    visible = layout[:, None, :] & exists[:, None, :] & causal[None, :, :]
    score_scale = 1.0 / math.sqrt(HEAD)

    def softmax_rows(query_side, key_side):
        query_blocks = query_side.astype(jnp.float32).reshape(QH, NB, BLK, HEAD)
        scores = jnp.einsum('hbqe,bke->hbqk', query_blocks, key_windows(key_side).astype(jnp.float32)) * score_scale
        scores = jnp.where(visible[None], scores, -jnp.inf)
        row_max = lax.optimization_barrier(jnp.max(scores, axis=-1, keepdims=True))
        exp_scores = jnp.exp(scores - row_max)
        return exp_scores / lax.optimization_barrier(jnp.sum(exp_scores, axis=-1, keepdims=True))
    new_probs = softmax_rows(query_pos, keys_pos)
    old_probs = softmax_rows(old_query_pos, old_keys_pos)
    score_grad = (KL_WEIGHT * score_scale * (new_probs - old_probs)).astype(jnp.bfloat16)
    score_grad = lax.optimization_barrier(score_grad).astype(jnp.float32)
    key_win = key_windows(keys_pos).astype(jnp.float32)
    query_grad = jnp.einsum('hbqk,bke->hbqe', score_grad, key_win).reshape(QH, TOKENS, HEAD).astype(jnp.bfloat16)
    query_blocks = query_pos.astype(jnp.float32).reshape(QH, NB, BLK, HEAD)
    key_win_grad = jnp.einsum('hbqk,hbqe->bke', score_grad, query_blocks).reshape(NB, BAND + 1, BLK, HEAD)
    key_grad_pad = jnp.zeros((NB + BAND, BLK, HEAD), jnp.float32)
    for shift_idx in range(BAND + 1):
        key_grad_pad = key_grad_pad.at[shift_idx:shift_idx + NB].add(key_win_grad[:, shift_idx])
    key_gradient = key_grad_pad[BAND:].reshape(TOKENS, HEAD).astype(jnp.bfloat16)
    pos_order = position_of_row()
    query_grad_rows = jnp.transpose(query_grad[:, pos_order], (1, 0, 2)).astype(jnp.float32)
    key_grad_rows = key_gradient[pos_order]
    weight_heads = w_query.astype(jnp.float32).reshape(D, QH, HEAD)
    normed_grad = jnp.einsum('the,dhe->td', query_grad_rows, weight_heads)
    normed_grad = normed_grad + jnp.dot(key_grad_rows, w_key.T, preferred_element_type=jnp.float32)
    normed_grad = normed_grad.astype(jnp.bfloat16)
    normed_grad = lax.optimization_barrier(normed_grad).astype(jnp.float32)
    inner_sum = lax.optimization_barrier(jnp.sum(normed_grad * gain_f32[None, :] * resid_f32, axis=1))
    resid_grad = gain_f32[None, :] * inv_rms[:, None] * normed_grad - resid_f32 * (inv_rms * inv_rms * inv_rms * inner_sum / D)[:, None]
    grad_blocks = resid_grad.reshape(TOKENS // step_rows, step_rows, D)

    def grad_block(index_gradient_pair):
        decoder_weight_rows = jnp.take(decoder, index_gradient_pair[0], axis=0).astype(jnp.float32)
        return jnp.einsum('ih,ich->ic', index_gradient_pair[1], decoder_weight_rows, precision=lax.Precision.HIGHEST)
    return lax.map(grad_block, (idx_blocks, grad_blocks)).reshape(TOKENS, TOPK)
```

```python
import math

import jax
import jax.numpy as jnp
from jax import lax
from jax.experimental import pallas as pl
from jax.experimental.pallas import tpu as pltpu
from jax.sharding import PartitionSpec as P

KL_WEIGHT = 16.0
EPSILON = 1e-05


def passed_along(array, axis, by):
    devices = lax.axis_size(axis)
    pairs = [(i, i + by) for i in range(devices) if 0 <= i + by < devices]
    return lax.ppermute(array, axis, pairs)


LATENTS_PER_ROW = 4
LANES = 128
PAIR_BLOCK = 2048
CONVERT_ROWS = 256
UNROLL = 32


def gather_kernel(idx_ref, block_ref, out_ref, table, picked):
    step = pl.program_id(1)
    rows = block_ref.shape[0]

    @pl.when(step < LATENTS_PER_ROW)
    def _():
        def convert(i, carry):
            at = pl.multiple_of(i * CONVERT_ROWS, CONVERT_ROWS)
            table[pl.ds(step * rows + at, CONVERT_ROWS), :] = block_ref[
                pl.ds(at, CONVERT_ROWS), :
            ].astype(jnp.float32)
            return carry

        lax.fori_loop(0, rows // CONVERT_ROWS, convert, 0)

    @pl.when(step >= LATENTS_PER_ROW)
    def _():
        first = (step - LATENTS_PER_ROW) * PAIR_BLOCK

        def pick(i, carry):
            at = pl.multiple_of(i * UNROLL, UNROLL)
            loaded = [table[pl.ds(idx_ref[first + at + k], 1), :] for k in range(UNROLL)]
            for k in range(UNROLL):
                picked[pl.ds(at + k, 1), :] = loaded[k]
            return carry

        lax.fori_loop(0, PAIR_BLOCK // UNROLL, pick, 0)
        out_ref[...] = picked[...].astype(out_ref.dtype)


def gather_rows(decoder, all_idx):
    rows, wide = decoder.shape
    features = wide // LATENTS_PER_ROW
    parts = features // LANES
    pairs = all_idx.size
    flat = all_idx.reshape(pairs)
    table_row = (flat % LATENTS_PER_ROW) * rows + flat // LATENTS_PER_ROW

    def in_block(part, step, idx_ref):
        loading = step < LATENTS_PER_ROW
        following = jnp.minimum(part + 1, parts - 1)
        return (0, jnp.where(loading, step * parts + part, following))

    def out_block(part, step, idx_ref):
        return (jnp.maximum(step - LATENTS_PER_ROW, 0), part)

    return pl.pallas_call(
        gather_kernel,
        out_shape=jax.ShapeDtypeStruct((pairs, features), decoder.dtype),
        grid_spec=pltpu.PrefetchScalarGridSpec(
            num_scalar_prefetch=1,
            grid=(parts, LATENTS_PER_ROW + pairs // PAIR_BLOCK),
            in_specs=[pl.BlockSpec((rows, LANES), in_block)],
            out_specs=pl.BlockSpec((PAIR_BLOCK, LANES), out_block),
            scratch_shapes=[
                pltpu.VMEM((LATENTS_PER_ROW * rows, LANES), jnp.float32),
                pltpu.VMEM((PAIR_BLOCK, LANES), jnp.float32),
            ],
        ),
        compiler_params=pltpu.CompilerParams(vmem_limit_bytes=52 * 1024 * 1024),
    )(table_row, decoder)


def decode_rows(decoder, all_idx, every_code_value, decoder_offset_bias):
    tokens, top_count = all_idx.shape
    step_rows = math.gcd(tokens, 1024)
    idx_blocks = all_idx.reshape(tokens // step_rows, step_rows, top_count)
    val_blocks = every_code_value.reshape(tokens // step_rows, step_rows, top_count)

    def decode_one_block(index_value_pair):
        decoder_weight_rows = jnp.take(decoder, index_value_pair[0], axis=0)
        return jnp.einsum(
            "bk,bkc->bc",
            index_value_pair[1],
            decoder_weight_rows,
            preferred_element_type=jnp.float32,
        )

    summed = lax.map(decode_one_block, (idx_blocks, val_blocks)).reshape(tokens, decoder.shape[1])
    return summed + decoder_offset_bias.astype(jnp.float32)[None, :]


def code_grads(decoder, all_idx, resid_grad):
    tokens, top_count = all_idx.shape
    step_rows = math.gcd(tokens, 1024)
    idx_blocks = all_idx.reshape(tokens // step_rows, step_rows, top_count)
    grad_blocks = resid_grad.reshape(tokens // step_rows, step_rows, resid_grad.shape[1])

    def code_one_block(index_gradient_pair):
        decoder_weight_rows = jnp.take(decoder, index_gradient_pair[0], axis=0)
        upper = lax.optimization_barrier(index_gradient_pair[1].astype(jnp.bfloat16))
        lower = (index_gradient_pair[1] - upper.astype(jnp.float32)).astype(jnp.bfloat16)
        first = jnp.einsum(
            "bc,bkc->bk", upper, decoder_weight_rows, preferred_element_type=jnp.float32
        )
        second_member = jnp.einsum(
            "bc,bkc->bk", lower, decoder_weight_rows, preferred_element_type=jnp.float32
        )
        return first + second_member

    return lax.map(code_one_block, (idx_blocks, grad_blocks)).reshape(tokens, top_count)


def attend(query_new, query_old, keys_new, keys_old, mask_layout, first_pos, block_len):
    range_len = query_new.shape[0]
    band_blocks = mask_layout.shape[1] - 1
    score_scale = 1.0 / math.sqrt(query_new.shape[1])
    query_at = first_pos + jnp.arange(range_len, dtype=jnp.int32)
    key_at = first_pos - range_len + jnp.arange(2 * range_len, dtype=jnp.int32)
    query_block = jnp.floor_divide(query_at, block_len)
    key_block = jnp.floor_divide(key_at, block_len)
    rel_slot = key_block[None, :] - query_block[:, None] + band_blocks
    layout_rows = lax.dynamic_slice_in_dim(
        mask_layout, first_pos // block_len, range_len // block_len, 0
    )
    layout_rows = jnp.repeat(layout_rows, block_len, axis=0)
    slot_ids = jnp.arange(band_blocks + 1, dtype=jnp.int32)
    layout_bit = jnp.sum(
        jnp.where(rel_slot[:, :, None] == slot_ids[None, None, :], layout_rows[:, None, :], 0),
        axis=2,
    )
    visible = (layout_bit > 0) & (key_block[None, :] >= 0) & (key_at[None, :] <= query_at[:, None])

    def softmax_rows(query_side, key_side):
        scores = (
            jnp.einsum("qe,ke->qk", query_side, key_side, preferred_element_type=jnp.float32)
            * score_scale
        )
        scores = jnp.where(visible, scores, -jnp.inf)
        row_max = jnp.max(scores, axis=1, keepdims=True)
        exp_scores = jnp.exp(scores - row_max)
        return exp_scores / jnp.sum(exp_scores, axis=1, keepdims=True)

    new_probs = softmax_rows(query_new, keys_new)
    old_probs = softmax_rows(query_old, keys_old)
    score_grad = (KL_WEIGHT * score_scale * (new_probs - old_probs)).astype(jnp.bfloat16)
    query_grad = jnp.einsum("qk,ke->qe", score_grad, keys_new, preferred_element_type=jnp.float32)
    key_gradient = jnp.einsum(
        "qk,qe->ke", score_grad, query_new, preferred_element_type=jnp.float32
    )
    return (query_grad.astype(jnp.bfloat16), key_gradient[:range_len], key_gradient[range_len:])


def local(
    codes_idx,
    codes_val,
    decoder,
    decoder_offset_bias,
    norm_gain,
    w_query,
    w_key,
    orig_queries,
    orig_keys,
    mask_layout,
):
    seq_count = lax.axis_size("seq")
    seq_index = lax.axis_index("seq")
    tok_rows = codes_idx.shape[0]
    heads_here = orig_queries.shape[0]
    head_dim = orig_keys.shape[1]
    all_heads = w_query.shape[1] // head_dim
    model_width = decoder_offset_bias.shape[0] * seq_count * lax.axis_size("lat")
    ranges = seq_count // heads_here
    range_len = tok_rows * heads_here
    block_len = tok_rows * seq_count // mask_layout.shape[0]
    flat_shape = (heads_here * tok_rows, head_dim)
    all_idx, every_code_value = (
        lax.all_gather(codes_idx, "seq", axis=0, tiled=True),
        lax.all_gather(codes_val, "seq", axis=0, tiled=True),
    )
    features = decoder_offset_bias.shape[0]
    picked_rows = None
    if features % LANES == 0:
        picked_rows = gather_rows(decoder[0], all_idx).reshape(*all_idx.shape, features)
        residual = jnp.einsum(
            "bk,bkc->bc", every_code_value, picked_rows, preferred_element_type=jnp.float32
        )
        residual = residual + decoder_offset_bias.astype(jnp.float32)[None, :]
    else:
        dec_local = decoder.reshape(decoder.shape[1] * LATENTS_PER_ROW, features)
        residual = decode_rows(dec_local, all_idx, every_code_value, decoder_offset_bias)
    residual = residual.astype(jnp.bfloat16)
    resid_f32 = residual.astype(jnp.float32)
    squares = lax.psum(jnp.sum(resid_f32 * resid_f32, axis=1), ("seq", "lat"))
    inv_rms = lax.rsqrt(squares / model_width + EPSILON)
    gain_f32 = norm_gain.astype(jnp.float32)
    normed = (resid_f32 * inv_rms[:, None] * gain_f32[None, :]).astype(jnp.bfloat16)
    local_rows = lax.all_to_all(normed, "seq", split_axis=0, concat_axis=1, tiled=True)
    wq_rows, wk_rows = (
        lax.all_gather(w_query, "seq", axis=0, tiled=True),
        lax.all_gather(w_key, "seq", axis=0, tiled=True),
    )
    wq_heads = wq_rows.reshape(wq_rows.shape[0], all_heads, head_dim)
    query_part = jnp.einsum("td,dhe->hte", local_rows, wq_heads, preferred_element_type=jnp.float32)
    key_part = jnp.dot(local_rows, wk_rows, preferred_element_type=jnp.float32)
    query_mine = lax.psum_scatter(query_part, "lat", scatter_dimension=0, tiled=True)
    key_full = lax.psum(key_part, "lat")
    query_send = query_mine.astype(jnp.bfloat16).reshape(flat_shape)
    old_send = orig_queries.reshape(flat_shape)
    key_many = jnp.broadcast_to(
        key_full.astype(jnp.bfloat16)[None], (heads_here, tok_rows, head_dim)
    )
    old_many = jnp.broadcast_to(orig_keys[None], (heads_here, tok_rows, head_dim))
    first_pos = seq_index % ranges * range_len
    query_new, query_old, keys_new, keys_old = (
        lax.all_to_all(query_send, "seq", split_axis=0, concat_axis=0, tiled=True),
        lax.all_to_all(old_send, "seq", split_axis=0, concat_axis=0, tiled=True),
        lax.all_to_all(
            key_many.reshape(flat_shape), "seq", split_axis=0, concat_axis=0, tiled=True
        ),
        lax.all_to_all(
            old_many.reshape(flat_shape), "seq", split_axis=0, concat_axis=0, tiled=True
        ),
    )
    prev_new, prev_old = passed_along((keys_new, keys_old), "seq", 1)
    query_grad, key_grad_prev, key_grad_own = attend(
        query_new,
        query_old,
        jnp.concatenate([prev_new, keys_new], axis=0),
        jnp.concatenate([prev_old, keys_old], axis=0),
        mask_layout,
        first_pos,
        block_len,
    )
    query_grad_wide = query_grad.astype(jnp.float32)
    key_next = passed_along(key_grad_prev.astype(jnp.bfloat16), "seq", -1).astype(
        key_grad_prev.dtype
    )
    query_back, key_back = (
        lax.all_to_all(
            query_grad_wide.astype(jnp.bfloat16), "seq", split_axis=0, concat_axis=0, tiled=True
        ).astype(query_grad_wide.dtype),
        lax.all_to_all(
            (key_grad_own + key_next).astype(jnp.bfloat16),
            "seq",
            split_axis=0,
            concat_axis=0,
            tiled=True,
        ).astype(jnp.float32),
    )
    key_local = jnp.sum(key_back.reshape(heads_here, tok_rows, head_dim), axis=0)
    key_total = lax.psum(key_local.astype(jnp.bfloat16), "lat")
    query_heads_grad = query_back.astype(jnp.bfloat16).reshape(heads_here, tok_rows, head_dim)
    query_all = lax.all_gather(query_heads_grad, "lat", axis=0, tiled=True)
    normed_grad = jnp.einsum("hte,dhe->td", query_all, wq_heads, preferred_element_type=jnp.float32)
    normed_grad = normed_grad + jnp.einsum(
        "te,de->td", key_total, wk_rows, preferred_element_type=jnp.float32
    )
    normed_grad = normed_grad.astype(jnp.bfloat16)
    grad_cols = lax.all_to_all(normed_grad, "seq", split_axis=1, concat_axis=0, tiled=True).astype(
        jnp.float32
    )
    inner_sum = lax.psum(jnp.sum(grad_cols * gain_f32[None, :] * resid_f32, axis=1), ("seq", "lat"))
    resid_grad = (
        gain_f32[None, :] * inv_rms[:, None] * grad_cols
        - resid_f32 * (inv_rms * inv_rms * inv_rms * inner_sum / model_width)[:, None]
    )
    if picked_rows is not None:
        grad_part = jnp.einsum(
            "bc,bkc->bk",
            resid_grad.astype(jnp.bfloat16),
            picked_rows,
            preferred_element_type=jnp.float32,
        )
    else:
        grad_part = code_grads(dec_local, all_idx, resid_grad)
    grad_seq = lax.psum_scatter(grad_part, "seq", scatter_dimension=0, tiled=True)
    return lax.psum(grad_seq, "lat")


def solution(mesh):
    in_specs = (
        P(("grp", "seq"), None),
        P(("grp", "seq"), None),
        P(("seq", "lat"), None, None),
        P(("seq", "lat")),
        P(("seq", "lat")),
        P(("seq", "lat"), None),
        P(("seq", "lat"), None),
        P("lat", ("grp", "seq"), None),
        P(("grp", "seq"), None),
        P("grp", None),
    )
    out_specs = P(("grp", "seq"), None)
    return jax.shard_map(local, mesh=mesh, in_specs=in_specs, out_specs=out_specs, check_vma=False)
```

```python
import functools
import math

import jax
import jax.numpy as jnp
from jax import lax
from jax.experimental import pallas as pl
from jax.experimental.pallas import tpu as pltpu
from jax.sharding import PartitionSpec as P

KL_WEIGHT = 16.0
EPSILON = 1e-05


def passed_along(array, axis, by):
    devices = lax.axis_size(axis)
    pairs = [(i, i + by) for i in range(devices) if 0 <= i + by < devices]
    return lax.ppermute(array, axis, pairs)


LATENTS_PER_ROW = 4
LANES = 128
PAIR_BLOCK = 2048
CONVERT_ROWS = 256
UNROLL = 32


def gather_kernel(idx_ref, block_ref, out_ref, table, picked):
    step = pl.program_id(1)
    rows = block_ref.shape[0]

    @pl.when(step < LATENTS_PER_ROW)
    def _():
        def convert(i, carry):
            at = pl.multiple_of(i * CONVERT_ROWS, CONVERT_ROWS)
            table[pl.ds(step * rows + at, CONVERT_ROWS), :] = block_ref[
                pl.ds(at, CONVERT_ROWS), :
            ].astype(jnp.float32)
            return carry

        lax.fori_loop(0, rows // CONVERT_ROWS, convert, 0)

    @pl.when(step >= LATENTS_PER_ROW)
    def _():
        first = (step - LATENTS_PER_ROW) * PAIR_BLOCK

        def pick(i, carry):
            at = pl.multiple_of(i * UNROLL, UNROLL)
            loaded = [table[pl.ds(idx_ref[first + at + k], 1), :] for k in range(UNROLL)]
            for k in range(UNROLL):
                picked[pl.ds(at + k, 1), :] = loaded[k]
            return carry

        lax.fori_loop(0, PAIR_BLOCK // UNROLL, pick, 0)
        out_ref[...] = picked[...].astype(out_ref.dtype)


def gather_rows(decoder, all_idx):
    rows, wide = decoder.shape
    features = wide // LATENTS_PER_ROW
    parts = features // LANES
    pairs = all_idx.size
    flat = all_idx.reshape(pairs)
    table_row = (flat % LATENTS_PER_ROW) * rows + flat // LATENTS_PER_ROW

    def in_block(part, step, idx_ref):
        loading = step < LATENTS_PER_ROW
        following = jnp.minimum(part + 1, parts - 1)
        return (0, jnp.where(loading, step * parts + part, following))

    def out_block(part, step, idx_ref):
        return (jnp.maximum(step - LATENTS_PER_ROW, 0), part)

    return pl.pallas_call(
        gather_kernel,
        out_shape=jax.ShapeDtypeStruct((pairs, features), decoder.dtype),
        grid_spec=pltpu.PrefetchScalarGridSpec(
            num_scalar_prefetch=1,
            grid=(parts, LATENTS_PER_ROW + pairs // PAIR_BLOCK),
            in_specs=[pl.BlockSpec((rows, LANES), in_block)],
            out_specs=pl.BlockSpec((PAIR_BLOCK, LANES), out_block),
            scratch_shapes=[
                pltpu.VMEM((LATENTS_PER_ROW * rows, LANES), jnp.float32),
                pltpu.VMEM((PAIR_BLOCK, LANES), jnp.float32),
            ],
        ),
        compiler_params=pltpu.CompilerParams(vmem_limit_bytes=52 * 1024 * 1024),
    )(table_row, decoder)


def decode_rows(decoder, all_idx, every_code_value, decoder_offset_bias):
    tokens, top_count = all_idx.shape
    step_rows = math.gcd(tokens, 1024)
    idx_blocks = all_idx.reshape(tokens // step_rows, step_rows, top_count)
    val_blocks = every_code_value.reshape(tokens // step_rows, step_rows, top_count)

    def decode_one_block(index_value_pair):
        decoder_weight_rows = jnp.take(decoder, index_value_pair[0], axis=0)
        return jnp.einsum(
            "bk,bkc->bc",
            index_value_pair[1],
            decoder_weight_rows,
            preferred_element_type=jnp.float32,
        )

    summed = lax.map(decode_one_block, (idx_blocks, val_blocks)).reshape(tokens, decoder.shape[1])
    return summed + decoder_offset_bias.astype(jnp.float32)[None, :]


def code_grads(decoder, all_idx, resid_grad):
    tokens, top_count = all_idx.shape
    step_rows = math.gcd(tokens, 1024)
    idx_blocks = all_idx.reshape(tokens // step_rows, step_rows, top_count)
    grad_blocks = resid_grad.reshape(tokens // step_rows, step_rows, resid_grad.shape[1])

    def code_one_block(index_gradient_pair):
        decoder_weight_rows = jnp.take(decoder, index_gradient_pair[0], axis=0)
        upper = lax.optimization_barrier(index_gradient_pair[1].astype(jnp.bfloat16))
        lower = (index_gradient_pair[1] - upper.astype(jnp.float32)).astype(jnp.bfloat16)
        first = jnp.einsum(
            "bc,bkc->bk", upper, decoder_weight_rows, preferred_element_type=jnp.float32
        )
        second_member = jnp.einsum(
            "bc,bkc->bk", lower, decoder_weight_rows, preferred_element_type=jnp.float32
        )
        return first + second_member

    return lax.map(code_one_block, (idx_blocks, grad_blocks)).reshape(tokens, top_count)


def attend(query_new, query_old, keys_new, keys_old, mask_layout, first_pos, block_len):
    range_len = query_new.shape[0]
    band_blocks = mask_layout.shape[1] - 1
    score_scale = 1.0 / math.sqrt(query_new.shape[1])
    query_at = first_pos + jnp.arange(range_len, dtype=jnp.int32)
    key_at = first_pos - range_len + jnp.arange(2 * range_len, dtype=jnp.int32)
    query_block = jnp.floor_divide(query_at, block_len)
    key_block = jnp.floor_divide(key_at, block_len)
    rel_slot = key_block[None, :] - query_block[:, None] + band_blocks
    layout_rows = lax.dynamic_slice_in_dim(
        mask_layout, first_pos // block_len, range_len // block_len, 0
    )
    layout_rows = jnp.repeat(layout_rows, block_len, axis=0)
    slot_ids = jnp.arange(band_blocks + 1, dtype=jnp.int32)
    layout_bit = jnp.sum(
        jnp.where(rel_slot[:, :, None] == slot_ids[None, None, :], layout_rows[:, None, :], 0),
        axis=2,
    )
    visible = (layout_bit > 0) & (key_block[None, :] >= 0) & (key_at[None, :] <= query_at[:, None])

    def softmax_rows(query_side, key_side):
        scores = (
            jnp.einsum("qe,ke->qk", query_side, key_side, preferred_element_type=jnp.float32)
            * score_scale
        )
        scores = jnp.where(visible, scores, -jnp.inf)
        row_max = jnp.max(scores, axis=1, keepdims=True)
        exp_scores = jnp.exp(scores - row_max)
        return exp_scores / jnp.sum(exp_scores, axis=1, keepdims=True)

    new_probs = softmax_rows(query_new, keys_new)
    old_probs = softmax_rows(query_old, keys_old)
    score_grad = (KL_WEIGHT * score_scale * (new_probs - old_probs)).astype(jnp.bfloat16)
    query_grad = jnp.einsum("qk,ke->qe", score_grad, keys_new, preferred_element_type=jnp.float32)
    key_gradient = jnp.einsum(
        "qk,qe->ke", score_grad, query_new, preferred_element_type=jnp.float32
    )
    return (query_grad.astype(jnp.bfloat16), key_gradient[:range_len], key_gradient[range_len:])


def local_any(
    codes_idx,
    codes_val,
    decoder,
    decoder_offset_bias,
    norm_gain,
    w_query,
    w_key,
    orig_queries,
    orig_keys,
    mask_layout,
):
    seq_count = lax.axis_size("seq")
    seq_index = lax.axis_index("seq")
    tok_rows = codes_idx.shape[0]
    heads_here = orig_queries.shape[0]
    head_dim = orig_keys.shape[1]
    all_heads = w_query.shape[1] // head_dim
    model_width = decoder_offset_bias.shape[0] * seq_count * lax.axis_size("lat")
    ranges = seq_count // heads_here
    range_len = tok_rows * heads_here
    block_len = tok_rows * seq_count // mask_layout.shape[0]
    flat_shape = (heads_here * tok_rows, head_dim)
    all_idx, every_code_value = (
        lax.all_gather(codes_idx, "seq", axis=0, tiled=True),
        lax.all_gather(codes_val, "seq", axis=0, tiled=True),
    )
    features = decoder_offset_bias.shape[0]
    dec_local = decoder.reshape(decoder.shape[1] * LATENTS_PER_ROW, features)
    residual = decode_rows(dec_local, all_idx, every_code_value, decoder_offset_bias)
    residual = residual.astype(jnp.bfloat16)
    resid_f32 = residual.astype(jnp.float32)
    squares = lax.psum(jnp.sum(resid_f32 * resid_f32, axis=1), ("seq", "lat"))
    inv_rms = lax.rsqrt(squares / model_width + EPSILON)
    gain_f32 = norm_gain.astype(jnp.float32)
    normed = (resid_f32 * inv_rms[:, None] * gain_f32[None, :]).astype(jnp.bfloat16)
    local_rows = lax.all_to_all(normed, "seq", split_axis=0, concat_axis=1, tiled=True)
    wq_rows, wk_rows = (
        lax.all_gather(w_query, "seq", axis=0, tiled=True),
        lax.all_gather(w_key, "seq", axis=0, tiled=True),
    )
    wq_heads = wq_rows.reshape(wq_rows.shape[0], all_heads, head_dim)
    query_part = jnp.einsum("td,dhe->hte", local_rows, wq_heads, preferred_element_type=jnp.float32)
    key_part = jnp.dot(local_rows, wk_rows, preferred_element_type=jnp.float32)
    query_mine = lax.psum_scatter(query_part, "lat", scatter_dimension=0, tiled=True)
    key_full = lax.psum(key_part, "lat")
    query_send = query_mine.astype(jnp.bfloat16).reshape(flat_shape)
    old_send = orig_queries.reshape(flat_shape)
    key_many = jnp.broadcast_to(
        key_full.astype(jnp.bfloat16)[None], (heads_here, tok_rows, head_dim)
    )
    old_many = jnp.broadcast_to(orig_keys[None], (heads_here, tok_rows, head_dim))
    first_pos = seq_index % ranges * range_len
    query_new, query_old, keys_new, keys_old = (
        lax.all_to_all(query_send, "seq", split_axis=0, concat_axis=0, tiled=True),
        lax.all_to_all(old_send, "seq", split_axis=0, concat_axis=0, tiled=True),
        lax.all_to_all(
            key_many.reshape(flat_shape), "seq", split_axis=0, concat_axis=0, tiled=True
        ),
        lax.all_to_all(
            old_many.reshape(flat_shape), "seq", split_axis=0, concat_axis=0, tiled=True
        ),
    )
    prev_new, prev_old = passed_along((keys_new, keys_old), "seq", 1)
    query_grad, key_grad_prev, key_grad_own = attend(
        query_new,
        query_old,
        jnp.concatenate([prev_new, keys_new], axis=0),
        jnp.concatenate([prev_old, keys_old], axis=0),
        mask_layout,
        first_pos,
        block_len,
    )
    query_grad_wide = query_grad.astype(jnp.float32)
    key_next = passed_along(key_grad_prev.astype(jnp.bfloat16), "seq", -1).astype(
        key_grad_prev.dtype
    )
    query_back, key_back = (
        lax.all_to_all(
            query_grad_wide.astype(jnp.bfloat16), "seq", split_axis=0, concat_axis=0, tiled=True
        ).astype(query_grad_wide.dtype),
        lax.all_to_all(
            (key_grad_own + key_next).astype(jnp.bfloat16),
            "seq",
            split_axis=0,
            concat_axis=0,
            tiled=True,
        ).astype(jnp.float32),
    )
    key_local = jnp.sum(key_back.reshape(heads_here, tok_rows, head_dim), axis=0)
    key_total = lax.psum(key_local.astype(jnp.bfloat16), "lat")
    query_heads_grad = query_back.astype(jnp.bfloat16).reshape(heads_here, tok_rows, head_dim)
    query_all = lax.all_gather(query_heads_grad, "lat", axis=0, tiled=True)
    normed_grad = jnp.einsum("hte,dhe->td", query_all, wq_heads, preferred_element_type=jnp.float32)
    normed_grad = normed_grad + jnp.einsum(
        "te,de->td", key_total, wk_rows, preferred_element_type=jnp.float32
    )
    normed_grad = normed_grad.astype(jnp.bfloat16)
    grad_cols = lax.all_to_all(normed_grad, "seq", split_axis=1, concat_axis=0, tiled=True).astype(
        jnp.float32
    )
    inner_sum = lax.psum(jnp.sum(grad_cols * gain_f32[None, :] * resid_f32, axis=1), ("seq", "lat"))
    resid_grad = (
        gain_f32[None, :] * inv_rms[:, None] * grad_cols
        - resid_f32 * (inv_rms * inv_rms * inv_rms * inner_sum / model_width)[:, None]
    )
    grad_part = code_grads(dec_local, all_idx, resid_grad)
    grad_seq = lax.psum_scatter(grad_part, "seq", scatter_dimension=0, tiled=True)
    return lax.psum(grad_seq, "lat")


def exchange_kernel(axes, lanes_of, count, kinds, *refs):
    sources, results = refs[:count], refs[count : 2 * count]
    send_sem, recv_sem, local_sem = refs[2 * count :]
    peers = math.prod(lanes_of)
    me = lax.axis_index(axes[0])
    if len(axes) > 1:
        me = me * lanes_of[1] + lax.axis_index(axes[1])

    def device(peer):
        if len(axes) > 1:
            return {axes[0]: peer // lanes_of[1], axes[1]: lax.rem(peer, lanes_of[1])}
        return {axes[0]: peer}

    def source(a, peer):
        if kinds[a] == "gather":
            return sources[a]
        return sources[a].at[peer // (peers // sources[a].shape[0])]

    barrier = pltpu.get_barrier_semaphore()
    for d in range(1, peers):
        pl.semaphore_signal(
            barrier,
            inc=1,
            device_id=device(lax.rem(me + d, peers)),
            device_id_type=pl.DeviceIdType.MESH,
        )
    own = [
        pltpu.make_async_copy(source(a, me), results[a].at[me], local_sem.at[a])
        for a in range(count)
    ]
    for copy in own:
        copy.start()
    pl.semaphore_wait(barrier, peers - 1)

    def remote(a, d, slot):
        peer = lax.rem(me + d, peers)
        return pltpu.make_async_remote_copy(
            src_ref=source(a, peer),
            dst_ref=results[a].at[slot],
            send_sem=send_sem.at[a, d],
            recv_sem=recv_sem.at[a, d],
            device_id=device(peer),
            device_id_type=pl.DeviceIdType.MESH,
        )

    for a in range(count):
        for d in range(1, peers):
            remote(a, d, me).start()
    for copy in own:
        copy.wait()
    for a in range(count):
        for d in range(1, peers):
            remote(a, d, lax.rem(me + peers - d, peers)).wait_recv()
    for a in range(count):
        for d in range(1, peers):
            remote(a, d, me).wait_send()


def exchange(axes, collective_id, *items):
    kinds = [kind for kind, _ in items]
    arrays = [array for _, array in items]
    sizes = [lax.axis_size(axis) for axis in axes]
    peers = math.prod(sizes)
    shapes = [
        jax.ShapeDtypeStruct((peers,) + (a.shape if kind == "gather" else a.shape[1:]), a.dtype)
        for kind, a in items
    ]
    count = len(items)
    return pl.pallas_call(
        functools.partial(exchange_kernel, axes, sizes, count, kinds),
        out_shape=shapes,
        in_specs=[pl.BlockSpec(memory_space=pltpu.VMEM)] * count,
        out_specs=[pl.BlockSpec(memory_space=pltpu.VMEM)] * count,
        scratch_shapes=[
            pltpu.SemaphoreType.DMA((count, peers)),
            pltpu.SemaphoreType.DMA((count, peers)),
            pltpu.SemaphoreType.DMA((count,)),
        ],
        compiler_params=pltpu.CompilerParams(
            collective_id=collective_id,
            has_side_effects=True,
            vmem_limit_bytes=32 * 1024 * 1024,
        ),
    )(*arrays)


def as_tile(vectors):
    missing = LANES - vectors.shape[-1]
    padded = jnp.pad(vectors, [(0, 0)] * (vectors.ndim - 1) + [(0, missing)])
    return jnp.broadcast_to(padded[..., None, :], padded.shape[:-1] + (8, LANES))


def local(
    codes_idx,
    codes_val,
    decoder,
    decoder_offset_bias,
    norm_gain,
    w_query,
    w_key,
    orig_queries,
    orig_keys,
    mask_layout,
):
    seq_count, lat_count = lax.axis_size("seq"), lax.axis_size("lat")
    features = decoder_offset_bias.shape[0]
    heads_here = orig_queries.shape[0]
    tok_rows, top_count = codes_idx.shape
    ranges = seq_count // heads_here
    if features % LANES or ranges != lat_count:
        return local_any(
            codes_idx,
            codes_val,
            decoder,
            decoder_offset_bias,
            norm_gain,
            w_query,
            w_key,
            orig_queries,
            orig_keys,
            mask_layout,
        )
    peers = seq_count * lat_count
    head_dim = orig_keys.shape[1]
    all_heads = heads_here * lat_count
    model_width = features * peers
    tokens = tok_rows * seq_count
    range_len = tokens // ranges
    sub = tok_rows // ranges
    block_len = tokens // mask_layout.shape[0]
    this_range = lax.axis_index("seq") % ranges
    both = ("seq", "lat")

    def by_position(array):
        cut = array.reshape(seq_count, ranges, sub, *array.shape[1:])
        return jnp.swapaxes(cut, 0, 1).reshape(array.shape)

    def by_token(array):
        cut = array.reshape(ranges, seq_count, sub, *array.shape[1:])
        return jnp.swapaxes(cut, 0, 1).reshape(array.shape)

    idx_all, val_all, query_old, keys_old = exchange(
        ("seq",),
        0,
        ("gather", codes_idx),
        ("gather", codes_val),
        ("scatter", orig_queries.reshape(seq_count, sub, head_dim)),
        ("gather", orig_keys),
    )
    idx_all = by_position(idx_all.reshape(tokens, top_count))
    val_all = by_position(val_all.reshape(tokens, top_count))
    query_old = query_old.reshape(range_len, head_dim)
    keys_old = by_position(keys_old.reshape(tokens, head_dim))

    picked_rows = gather_rows(decoder[0], idx_all).reshape(tokens, top_count, features)
    residual = jnp.einsum("bk,bkc->bc", val_all, picked_rows, preferred_element_type=jnp.float32)
    residual = (residual + decoder_offset_bias.astype(jnp.float32)[None, :]).astype(jnp.bfloat16)
    resid_f32 = residual.astype(jnp.float32)
    gain_f32 = norm_gain.astype(jnp.float32)
    squares = jnp.sum(resid_f32 * resid_f32, axis=1)
    scaled = (resid_f32 * gain_f32[None, :]).astype(jnp.bfloat16)

    query_part = jnp.dot(scaled, w_query, preferred_element_type=jnp.float32).astype(jnp.bfloat16)
    query_part = query_part.reshape(ranges, range_len, lat_count, heads_here, head_dim)
    query_part = jnp.transpose(query_part, (3, 0, 2, 1, 4)).reshape(peers, range_len, head_dim)
    key_part = jnp.dot(scaled, w_key, preferred_element_type=jnp.float32).astype(jnp.bfloat16)
    query_parts, key_parts, square_parts = exchange(
        both,
        1,
        ("scatter", query_part),
        ("scatter", by_token(key_part).reshape(peers, sub, head_dim)),
        ("scatter", as_tile(by_token(squares).reshape(peers, sub))),
    )
    query_raw = jnp.sum(query_parts.astype(jnp.float32), axis=0)
    key_raw = jnp.sum(key_parts.astype(jnp.float32), axis=0)
    inv_here = lax.rsqrt(jnp.sum(square_parts[:, 0, :sub], axis=0) / model_width + EPSILON)
    key_here = (key_raw * inv_here[:, None]).astype(jnp.bfloat16)
    keys_new, inv_tiles = exchange(both, 2, ("gather", key_here), ("gather", as_tile(inv_here)))
    keys_new = by_position(keys_new.reshape(tokens, head_dim))
    inv_rms = by_position(inv_tiles[:, 0, :sub].reshape(tokens))
    first_pos = this_range * range_len
    inv_range = lax.dynamic_slice_in_dim(inv_rms, first_pos, range_len, 0)
    query_new = (query_raw * inv_range[:, None]).astype(jnp.bfloat16)

    def window(keys):
        padded = jnp.pad(keys, ((range_len, 0), (0, 0)))
        return lax.dynamic_slice_in_dim(padded, first_pos, 2 * range_len, 0)

    query_grad, key_grad_prev, key_grad_own = attend(
        query_new,
        query_old,
        window(keys_new),
        window(keys_old),
        mask_layout,
        first_pos,
        block_len,
    )
    key_grad = lax.dynamic_update_slice_in_dim(
        jnp.zeros(((ranges + 1) * range_len, head_dim), jnp.float32),
        jnp.concatenate([key_grad_prev, key_grad_own], axis=0),
        first_pos,
        0,
    )[range_len:]
    query_inner = jnp.sum(query_grad.astype(jnp.float32) * query_new.astype(jnp.float32), axis=1)
    query_grads, key_grad_parts, inner_parts = exchange(
        both,
        3,
        ("gather", query_grad),
        ("scatter", by_token(key_grad.astype(jnp.bfloat16)).reshape(peers, sub, head_dim)),
        ("gather", query_inner.reshape(range_len // LANES, LANES)),
    )
    key_grad_here = jnp.sum(key_grad_parts.astype(jnp.float32), axis=0).astype(jnp.bfloat16)
    (key_grads,) = exchange(both, 4, ("gather", key_grad_here))
    key_grads = by_position(key_grads.reshape(tokens, head_dim))

    inner = jnp.sum(
        inner_parts.reshape(heads_here, ranges, lat_count, range_len), axis=(0, 2)
    ).reshape(tokens)
    inner = inner + jnp.sum(key_grads.astype(jnp.float32) * keys_new.astype(jnp.float32), axis=1)
    query_grads = query_grads.reshape(heads_here, ranges, lat_count, range_len, head_dim)
    query_grads = jnp.transpose(query_grads, (1, 3, 2, 0, 4)).reshape(tokens, all_heads * head_dim)
    normed_grad = jnp.einsum("te,de->td", query_grads, w_query, preferred_element_type=jnp.float32)
    normed_grad = normed_grad + jnp.einsum(
        "te,de->td", key_grads, w_key, preferred_element_type=jnp.float32
    )
    resid_grad = (
        gain_f32[None, :] * inv_rms[:, None] * normed_grad
        - resid_f32 * (inv_rms * inv_rms * inner / model_width)[:, None]
    ).astype(jnp.bfloat16)
    grad_part = jnp.einsum("bc,bkc->bk", resid_grad, picked_rows, preferred_element_type=jnp.float32)
    grad_part = by_token(grad_part).reshape(seq_count, tok_rows * top_count // LANES, LANES)
    (grad_parts,) = exchange(both, 5, ("scatter", grad_part))
    return jnp.sum(grad_parts, axis=0).reshape(tok_rows, top_count)


def solution(mesh):
    in_specs = (
        P(("grp", "seq"), None),
        P(("grp", "seq"), None),
        P(("seq", "lat"), None, None),
        P(("seq", "lat")),
        P(("seq", "lat")),
        P(("seq", "lat"), None),
        P(("seq", "lat"), None),
        P("lat", ("grp", "seq"), None),
        P(("grp", "seq"), None),
        P("grp", None),
    )
    out_specs = P(("grp", "seq"), None)
    return jax.shard_map(local, mesh=mesh, in_specs=in_specs, out_specs=out_specs, check_vma=False)
```

```python
import functools
import math

import jax
import jax.numpy as jnp
from jax import lax
from jax.experimental import pallas as pl
from jax.experimental.pallas import tpu as pltpu
from jax.sharding import PartitionSpec as P

KL_WEIGHT = 16.0
EPSILON = 1e-05


def passed_along(array, axis, by):
    devices = lax.axis_size(axis)
    pairs = [(i, i + by) for i in range(devices) if 0 <= i + by < devices]
    return lax.ppermute(array, axis, pairs)


LATENTS_PER_ROW = 4
LANES = 128
PAIR_BLOCK = 2048
CONVERT_ROWS = 256
UNROLL = 32


def gather_kernel(idx_ref, block_ref, out_ref, table, picked):
    step = pl.program_id(1)
    rows = block_ref.shape[0]

    @pl.when(step < LATENTS_PER_ROW)
    def _():
        def convert(i, carry):
            at = pl.multiple_of(i * CONVERT_ROWS, CONVERT_ROWS)
            table[pl.ds(step * rows + at, CONVERT_ROWS), :] = block_ref[
                pl.ds(at, CONVERT_ROWS), :
            ].astype(jnp.float32)
            return carry

        lax.fori_loop(0, rows // CONVERT_ROWS, convert, 0)

    @pl.when(step >= LATENTS_PER_ROW)
    def _():
        first = (step - LATENTS_PER_ROW) * PAIR_BLOCK

        def pick(i, carry):
            at = pl.multiple_of(i * UNROLL, UNROLL)
            loaded = [table[pl.ds(idx_ref[first + at + k], 1), :] for k in range(UNROLL)]
            for k in range(UNROLL):
                picked[pl.ds(at + k, 1), :] = loaded[k]
            return carry

        lax.fori_loop(0, PAIR_BLOCK // UNROLL, pick, 0)
        out_ref[...] = picked[...].astype(out_ref.dtype)


def gather_rows(decoder, all_idx):
    rows, wide = decoder.shape
    features = wide // LATENTS_PER_ROW
    parts = features // LANES
    pairs = all_idx.size
    flat = all_idx.reshape(pairs)
    table_row = (flat % LATENTS_PER_ROW) * rows + flat // LATENTS_PER_ROW

    def in_block(part, step, idx_ref):
        loading = step < LATENTS_PER_ROW
        following = jnp.minimum(part + 1, parts - 1)
        return (0, jnp.where(loading, step * parts + part, following))

    def out_block(part, step, idx_ref):
        return (jnp.maximum(step - LATENTS_PER_ROW, 0), part)

    return pl.pallas_call(
        gather_kernel,
        out_shape=jax.ShapeDtypeStruct((pairs, features), decoder.dtype),
        grid_spec=pltpu.PrefetchScalarGridSpec(
            num_scalar_prefetch=1,
            grid=(parts, LATENTS_PER_ROW + pairs // PAIR_BLOCK),
            in_specs=[pl.BlockSpec((rows, LANES), in_block)],
            out_specs=pl.BlockSpec((PAIR_BLOCK, LANES), out_block),
            scratch_shapes=[
                pltpu.VMEM((LATENTS_PER_ROW * rows, LANES), jnp.float32),
                pltpu.VMEM((PAIR_BLOCK, LANES), jnp.float32),
            ],
        ),
        compiler_params=pltpu.CompilerParams(vmem_limit_bytes=52 * 1024 * 1024),
    )(table_row, decoder)


def decode_rows(decoder, all_idx, every_code_value, decoder_offset_bias):
    tokens, top_count = all_idx.shape
    step_rows = math.gcd(tokens, 1024)
    idx_blocks = all_idx.reshape(tokens // step_rows, step_rows, top_count)
    val_blocks = every_code_value.reshape(tokens // step_rows, step_rows, top_count)

    def decode_one_block(index_value_pair):
        decoder_weight_rows = jnp.take(decoder, index_value_pair[0], axis=0)
        return jnp.einsum(
            "bk,bkc->bc",
            index_value_pair[1],
            decoder_weight_rows,
            preferred_element_type=jnp.float32,
        )

    summed = lax.map(decode_one_block, (idx_blocks, val_blocks)).reshape(tokens, decoder.shape[1])
    return summed + decoder_offset_bias.astype(jnp.float32)[None, :]


def code_grads(decoder, all_idx, resid_grad):
    tokens, top_count = all_idx.shape
    step_rows = math.gcd(tokens, 1024)
    idx_blocks = all_idx.reshape(tokens // step_rows, step_rows, top_count)
    grad_blocks = resid_grad.reshape(tokens // step_rows, step_rows, resid_grad.shape[1])

    def code_one_block(index_gradient_pair):
        decoder_weight_rows = jnp.take(decoder, index_gradient_pair[0], axis=0)
        upper = lax.optimization_barrier(index_gradient_pair[1].astype(jnp.bfloat16))
        lower = (index_gradient_pair[1] - upper.astype(jnp.float32)).astype(jnp.bfloat16)
        first = jnp.einsum(
            "bc,bkc->bk", upper, decoder_weight_rows, preferred_element_type=jnp.float32
        )
        second_member = jnp.einsum(
            "bc,bkc->bk", lower, decoder_weight_rows, preferred_element_type=jnp.float32
        )
        return first + second_member

    return lax.map(code_one_block, (idx_blocks, grad_blocks)).reshape(tokens, top_count)


def attend(query_new, query_old, keys_new, keys_old, mask_layout, first_pos, block_len):
    range_len = query_new.shape[0]
    band_blocks = mask_layout.shape[1] - 1
    score_scale = 1.0 / math.sqrt(query_new.shape[1])
    query_at = first_pos + jnp.arange(range_len, dtype=jnp.int32)
    key_at = first_pos - range_len + jnp.arange(2 * range_len, dtype=jnp.int32)
    query_block = jnp.floor_divide(query_at, block_len)
    key_block = jnp.floor_divide(key_at, block_len)
    rel_slot = key_block[None, :] - query_block[:, None] + band_blocks
    layout_rows = lax.dynamic_slice_in_dim(
        mask_layout, first_pos // block_len, range_len // block_len, 0
    )
    layout_rows = jnp.repeat(layout_rows, block_len, axis=0)
    slot_ids = jnp.arange(band_blocks + 1, dtype=jnp.int32)
    layout_bit = jnp.sum(
        jnp.where(rel_slot[:, :, None] == slot_ids[None, None, :], layout_rows[:, None, :], 0),
        axis=2,
    )
    visible = (layout_bit > 0) & (key_block[None, :] >= 0) & (key_at[None, :] <= query_at[:, None])

    def softmax_rows(query_side, key_side):
        scores = (
            jnp.einsum("qe,ke->qk", query_side, key_side, preferred_element_type=jnp.float32)
            * score_scale
        )
        scores = jnp.where(visible, scores, -jnp.inf)
        row_max = jnp.max(scores, axis=1, keepdims=True)
        exp_scores = jnp.exp(scores - row_max)
        return exp_scores / jnp.sum(exp_scores, axis=1, keepdims=True)

    new_probs = softmax_rows(query_new, keys_new)
    old_probs = softmax_rows(query_old, keys_old)
    score_grad = (KL_WEIGHT * score_scale * (new_probs - old_probs)).astype(jnp.bfloat16)
    query_grad = jnp.einsum("qk,ke->qe", score_grad, keys_new, preferred_element_type=jnp.float32)
    key_gradient = jnp.einsum(
        "qk,qe->ke", score_grad, query_new, preferred_element_type=jnp.float32
    )
    return (query_grad.astype(jnp.bfloat16), key_gradient[:range_len], key_gradient[range_len:])


def local_any(
    codes_idx,
    codes_val,
    decoder,
    decoder_offset_bias,
    norm_gain,
    w_query,
    w_key,
    orig_queries,
    orig_keys,
    mask_layout,
):
    seq_count = lax.axis_size("seq")
    seq_index = lax.axis_index("seq")
    tok_rows = codes_idx.shape[0]
    heads_here = orig_queries.shape[0]
    head_dim = orig_keys.shape[1]
    all_heads = w_query.shape[1] // head_dim
    model_width = decoder_offset_bias.shape[0] * seq_count * lax.axis_size("lat")
    ranges = seq_count // heads_here
    range_len = tok_rows * heads_here
    block_len = tok_rows * seq_count // mask_layout.shape[0]
    flat_shape = (heads_here * tok_rows, head_dim)
    all_idx, every_code_value = (
        lax.all_gather(codes_idx, "seq", axis=0, tiled=True),
        lax.all_gather(codes_val, "seq", axis=0, tiled=True),
    )
    features = decoder_offset_bias.shape[0]
    dec_local = decoder.reshape(decoder.shape[1] * LATENTS_PER_ROW, features)
    residual = decode_rows(dec_local, all_idx, every_code_value, decoder_offset_bias)
    residual = residual.astype(jnp.bfloat16)
    resid_f32 = residual.astype(jnp.float32)
    squares = lax.psum(jnp.sum(resid_f32 * resid_f32, axis=1), ("seq", "lat"))
    inv_rms = lax.rsqrt(squares / model_width + EPSILON)
    gain_f32 = norm_gain.astype(jnp.float32)
    normed = (resid_f32 * inv_rms[:, None] * gain_f32[None, :]).astype(jnp.bfloat16)
    local_rows = lax.all_to_all(normed, "seq", split_axis=0, concat_axis=1, tiled=True)
    wq_rows, wk_rows = (
        lax.all_gather(w_query, "seq", axis=0, tiled=True),
        lax.all_gather(w_key, "seq", axis=0, tiled=True),
    )
    wq_heads = wq_rows.reshape(wq_rows.shape[0], all_heads, head_dim)
    query_part = jnp.einsum("td,dhe->hte", local_rows, wq_heads, preferred_element_type=jnp.float32)
    key_part = jnp.dot(local_rows, wk_rows, preferred_element_type=jnp.float32)
    query_mine = lax.psum_scatter(query_part, "lat", scatter_dimension=0, tiled=True)
    key_full = lax.psum(key_part, "lat")
    query_send = query_mine.astype(jnp.bfloat16).reshape(flat_shape)
    old_send = orig_queries.reshape(flat_shape)
    key_many = jnp.broadcast_to(
        key_full.astype(jnp.bfloat16)[None], (heads_here, tok_rows, head_dim)
    )
    old_many = jnp.broadcast_to(orig_keys[None], (heads_here, tok_rows, head_dim))
    first_pos = seq_index % ranges * range_len
    query_new, query_old, keys_new, keys_old = (
        lax.all_to_all(query_send, "seq", split_axis=0, concat_axis=0, tiled=True),
        lax.all_to_all(old_send, "seq", split_axis=0, concat_axis=0, tiled=True),
        lax.all_to_all(
            key_many.reshape(flat_shape), "seq", split_axis=0, concat_axis=0, tiled=True
        ),
        lax.all_to_all(
            old_many.reshape(flat_shape), "seq", split_axis=0, concat_axis=0, tiled=True
        ),
    )
    prev_new, prev_old = passed_along((keys_new, keys_old), "seq", 1)
    query_grad, key_grad_prev, key_grad_own = attend(
        query_new,
        query_old,
        jnp.concatenate([prev_new, keys_new], axis=0),
        jnp.concatenate([prev_old, keys_old], axis=0),
        mask_layout,
        first_pos,
        block_len,
    )
    query_grad_wide = query_grad.astype(jnp.float32)
    key_next = passed_along(key_grad_prev.astype(jnp.bfloat16), "seq", -1).astype(
        key_grad_prev.dtype
    )
    query_back, key_back = (
        lax.all_to_all(
            query_grad_wide.astype(jnp.bfloat16), "seq", split_axis=0, concat_axis=0, tiled=True
        ).astype(query_grad_wide.dtype),
        lax.all_to_all(
            (key_grad_own + key_next).astype(jnp.bfloat16),
            "seq",
            split_axis=0,
            concat_axis=0,
            tiled=True,
        ).astype(jnp.float32),
    )
    key_local = jnp.sum(key_back.reshape(heads_here, tok_rows, head_dim), axis=0)
    key_total = lax.psum(key_local.astype(jnp.bfloat16), "lat")
    query_heads_grad = query_back.astype(jnp.bfloat16).reshape(heads_here, tok_rows, head_dim)
    query_all = lax.all_gather(query_heads_grad, "lat", axis=0, tiled=True)
    normed_grad = jnp.einsum("hte,dhe->td", query_all, wq_heads, preferred_element_type=jnp.float32)
    normed_grad = normed_grad + jnp.einsum(
        "te,de->td", key_total, wk_rows, preferred_element_type=jnp.float32
    )
    normed_grad = normed_grad.astype(jnp.bfloat16)
    grad_cols = lax.all_to_all(normed_grad, "seq", split_axis=1, concat_axis=0, tiled=True).astype(
        jnp.float32
    )
    inner_sum = lax.psum(jnp.sum(grad_cols * gain_f32[None, :] * resid_f32, axis=1), ("seq", "lat"))
    resid_grad = (
        gain_f32[None, :] * inv_rms[:, None] * grad_cols
        - resid_f32 * (inv_rms * inv_rms * inv_rms * inner_sum / model_width)[:, None]
    )
    grad_part = code_grads(dec_local, all_idx, resid_grad)
    grad_seq = lax.psum_scatter(grad_part, "seq", scatter_dimension=0, tiled=True)
    return lax.psum(grad_seq, "lat")


def exchange_kernel(axes, lanes_of, count, kinds, *refs):
    sources, results = refs[:count], refs[count : 2 * count]
    send_sem, recv_sem, local_sem = refs[2 * count :]
    peers = math.prod(lanes_of)
    me = lax.axis_index(axes[0])
    if len(axes) > 1:
        me = me * lanes_of[1] + lax.axis_index(axes[1])

    def device(peer):
        if len(axes) > 1:
            return {axes[0]: peer // lanes_of[1], axes[1]: lax.rem(peer, lanes_of[1])}
        return {axes[0]: peer}

    def source(a, peer):
        if kinds[a] == "gather":
            return sources[a]
        return sources[a].at[peer // (peers // sources[a].shape[0])]

    barrier = pltpu.get_barrier_semaphore()
    for d in range(1, peers):
        pl.semaphore_signal(
            barrier,
            inc=1,
            device_id=device(lax.rem(me + d, peers)),
            device_id_type=pl.DeviceIdType.MESH,
        )
    own = [
        pltpu.make_async_copy(source(a, me), results[a].at[me], local_sem.at[a])
        for a in range(count)
    ]
    for copy in own:
        copy.start()
    pl.semaphore_wait(barrier, peers - 1)

    def remote(a, d, slot):
        peer = lax.rem(me + d, peers)
        return pltpu.make_async_remote_copy(
            src_ref=source(a, peer),
            dst_ref=results[a].at[slot],
            send_sem=send_sem.at[a, d],
            recv_sem=recv_sem.at[a, d],
            device_id=device(peer),
            device_id_type=pl.DeviceIdType.MESH,
        )

    for a in range(count):
        for d in range(1, peers):
            remote(a, d, me).start()
    for copy in own:
        copy.wait()
    for a in range(count):
        for d in range(1, peers):
            remote(a, d, lax.rem(me + peers - d, peers)).wait_recv()
    for a in range(count):
        for d in range(1, peers):
            remote(a, d, me).wait_send()


def exchange(axes, collective_id, *items):
    kinds = [kind for kind, _ in items]
    arrays = [array for _, array in items]
    sizes = [lax.axis_size(axis) for axis in axes]
    peers = math.prod(sizes)
    shapes = [
        jax.ShapeDtypeStruct((peers,) + (a.shape if kind == "gather" else a.shape[1:]), a.dtype)
        for kind, a in items
    ]
    count = len(items)
    return pl.pallas_call(
        functools.partial(exchange_kernel, axes, sizes, count, kinds),
        out_shape=shapes,
        in_specs=[pl.BlockSpec(memory_space=pltpu.VMEM)] * count,
        out_specs=[pl.BlockSpec(memory_space=pltpu.VMEM)] * count,
        scratch_shapes=[
            pltpu.SemaphoreType.DMA((count, peers)),
            pltpu.SemaphoreType.DMA((count, peers)),
            pltpu.SemaphoreType.DMA((count,)),
        ],
        compiler_params=pltpu.CompilerParams(
            collective_id=collective_id,
            has_side_effects=True,
            vmem_limit_bytes=32 * 1024 * 1024,
        ),
    )(*arrays)


def as_tile(vectors):
    missing = LANES - vectors.shape[-1]
    padded = jnp.pad(vectors, [(0, 0)] * (vectors.ndim - 1) + [(0, missing)])
    return jnp.broadcast_to(padded[..., None, :], padded.shape[:-1] + (8, LANES))


def local(
    codes_idx,
    codes_val,
    decoder,
    decoder_offset_bias,
    norm_gain,
    w_query,
    w_key,
    orig_queries,
    orig_keys,
    mask_layout,
):
    seq_count, lat_count = lax.axis_size("seq"), lax.axis_size("lat")
    features = decoder_offset_bias.shape[0]
    heads_here = orig_queries.shape[0]
    tok_rows, top_count = codes_idx.shape
    ranges = seq_count // heads_here
    if features % LANES or ranges != lat_count:
        return local_any(
            codes_idx,
            codes_val,
            decoder,
            decoder_offset_bias,
            norm_gain,
            w_query,
            w_key,
            orig_queries,
            orig_keys,
            mask_layout,
        )
    peers = seq_count * lat_count
    head_dim = orig_keys.shape[1]
    all_heads = heads_here * lat_count
    model_width = features * peers
    tokens = tok_rows * seq_count
    range_len = tokens // ranges
    sub = tok_rows // ranges
    block_len = tokens // mask_layout.shape[0]
    this_range = lax.axis_index("seq") % ranges
    both = ("seq", "lat")

    def by_position(array, sub=sub):
        cut = array.reshape(seq_count, ranges, sub, *array.shape[1:])
        return jnp.swapaxes(cut, 0, 1).reshape(array.shape)

    def by_token(array):
        cut = array.reshape(ranges, seq_count, sub, *array.shape[1:])
        return jnp.swapaxes(cut, 0, 1).reshape(array.shape)

    flat_rows = tok_rows * top_count // LANES
    old_half = lax.dynamic_slice_in_dim(orig_keys, lax.axis_index("lat") * sub, sub, 0)
    idx_all, val_all, query_old, old_half = exchange(
        ("seq",),
        0,
        ("gather", codes_idx.reshape(flat_rows, LANES)),
        ("gather", codes_val.reshape(flat_rows, LANES)),
        ("scatter", orig_queries.reshape(seq_count, sub, head_dim)),
        ("gather", old_half),
    )
    idx_all = by_position(idx_all.reshape(seq_count * flat_rows, LANES), flat_rows // ranges)
    val_all = by_position(val_all.reshape(seq_count * flat_rows, LANES), flat_rows // ranges)
    val_all = val_all.reshape(tokens, top_count)
    query_old = query_old.reshape(range_len, head_dim)

    picked_rows = gather_rows(decoder[0], idx_all).reshape(tokens, top_count, features)
    residual = jnp.einsum("bk,bkc->bc", val_all, picked_rows, preferred_element_type=jnp.float32)
    residual = (residual + decoder_offset_bias.astype(jnp.float32)[None, :]).astype(jnp.bfloat16)
    resid_f32 = residual.astype(jnp.float32)
    gain_f32 = norm_gain.astype(jnp.float32)
    squares = jnp.sum(resid_f32 * resid_f32, axis=1)
    scaled = (resid_f32 * gain_f32[None, :]).astype(jnp.bfloat16)

    wq_heads = w_query.reshape(features, all_heads, head_dim)
    query_part = jnp.einsum("td,dhe->hte", scaled, wq_heads, preferred_element_type=jnp.float32)
    key_part = jnp.dot(scaled, w_key, preferred_element_type=jnp.float32)
    query_pair, key_pair, square_pair, keys_old = exchange(
        ("lat",),
        1,
        ("scatter", query_part.astype(jnp.bfloat16).reshape(lat_count, -1, head_dim)),
        ("scatter", key_part.astype(jnp.bfloat16).reshape(lat_count, range_len, head_dim)),
        ("scatter", as_tile(squares.reshape(lat_count * seq_count, sub)).reshape(lat_count, -1, LANES)),
        ("gather", old_half.reshape(range_len, head_dim)),
    )
    keys_old = keys_old.reshape(tokens, head_dim)

    def pair_sum(array):
        return jnp.sum(array.astype(jnp.float32), axis=0).astype(array.dtype)

    query_parts, key_parts, square_parts = exchange(
        ("seq",),
        6,
        ("scatter", pair_sum(query_pair).reshape(seq_count, range_len, head_dim)),
        ("scatter", pair_sum(key_pair).reshape(seq_count, sub, head_dim)),
        ("scatter", pair_sum(square_pair).reshape(seq_count, 8, LANES)),
    )
    query_raw = jnp.sum(query_parts.astype(jnp.float32), axis=0)
    key_raw = jnp.sum(key_parts.astype(jnp.float32), axis=0)
    inv_here = lax.rsqrt(jnp.sum(square_parts[:, 0, :sub], axis=0) / model_width + EPSILON)
    key_here = (key_raw * inv_here[:, None]).astype(jnp.bfloat16)
    keys_new, inv_tiles = exchange(both, 2, ("gather", key_here), ("gather", as_tile(inv_here)))
    keys_new = by_position(keys_new.reshape(tokens, head_dim))
    inv_rms = by_position(inv_tiles[:, 0, :sub].reshape(tokens))
    first_pos = this_range * range_len
    inv_range = lax.dynamic_slice_in_dim(inv_rms, first_pos, range_len, 0)
    query_new = (query_raw * inv_range[:, None]).astype(jnp.bfloat16)

    def window(keys):
        padded = jnp.pad(keys, ((range_len, 0), (0, 0)))
        return lax.dynamic_slice_in_dim(padded, first_pos, 2 * range_len, 0)

    query_grad, key_grad_prev, key_grad_own = attend(
        query_new,
        query_old,
        window(keys_new),
        window(keys_old),
        mask_layout,
        first_pos,
        block_len,
    )
    key_grad = lax.dynamic_update_slice_in_dim(
        jnp.zeros(((ranges + 1) * range_len, head_dim), jnp.float32),
        jnp.concatenate([key_grad_prev, key_grad_own], axis=0),
        first_pos,
        0,
    )[range_len:]
    query_inner = jnp.sum(query_grad.astype(jnp.float32) * query_new.astype(jnp.float32), axis=1)
    query_grads, key_grad_parts, inner_parts = exchange(
        ("seq",),
        3,
        ("gather", query_grad),
        ("scatter", by_token(key_grad.astype(jnp.bfloat16)).reshape(seq_count, tok_rows, head_dim)),
        ("gather", query_inner.reshape(range_len // LANES, LANES)),
    )
    query_grads, key_grad_pair, inner_parts = exchange(
        ("lat",),
        7,
        ("gather", query_grads.reshape(-1, head_dim)),
        ("scatter", pair_sum(key_grad_parts).reshape(lat_count, sub, head_dim)),
        ("gather", inner_parts.reshape(-1, LANES)),
    )
    key_grad_here = pair_sum(key_grad_pair)
    (key_grads,) = exchange(both, 4, ("gather", key_grad_here))
    key_grads = by_position(key_grads.reshape(tokens, head_dim))

    inner = jnp.sum(inner_parts.reshape(all_heads, tokens), axis=0)
    inner = inner + jnp.sum(key_grads.astype(jnp.float32) * keys_new.astype(jnp.float32), axis=1)
    query_grads = query_grads.reshape(all_heads, tokens, head_dim)
    normed_grad = jnp.einsum("hte,dhe->td", query_grads, wq_heads, preferred_element_type=jnp.float32)
    normed_grad = normed_grad + jnp.einsum(
        "te,de->td", key_grads, w_key, preferred_element_type=jnp.float32
    )
    resid_grad = (
        gain_f32[None, :] * inv_rms[:, None] * normed_grad
        - resid_f32 * (inv_rms * inv_rms * inner / model_width)[:, None]
    ).astype(jnp.bfloat16)
    grad_part = jnp.einsum("bc,bkc->bk", resid_grad, picked_rows, preferred_element_type=jnp.float32)
    grad_part = by_token(grad_part.astype(jnp.bfloat16)).reshape(seq_count, flat_rows, LANES)
    (grad_parts,) = exchange(both, 5, ("scatter", grad_part))
    grad_parts = grad_parts.astype(jnp.float32)
    return jnp.sum(grad_parts, axis=0).reshape(tok_rows, top_count)


def solution(mesh):
    in_specs = (
        P(("grp", "seq"), None),
        P(("grp", "seq"), None),
        P(("seq", "lat"), None, None),
        P(("seq", "lat")),
        P(("seq", "lat")),
        P(("seq", "lat"), None),
        P(("seq", "lat"), None),
        P("lat", ("grp", "seq"), None),
        P(("grp", "seq"), None),
        P("grp", None),
    )
    out_specs = P(("grp", "seq"), None)
    return jax.shard_map(local, mesh=mesh, in_specs=in_specs, out_specs=out_specs, check_vma=False)
```

```python
import functools
import math

import jax
import jax.numpy as jnp
from jax import lax
from jax.experimental import pallas as pl
from jax.experimental.pallas import tpu as pltpu
from jax.sharding import PartitionSpec as P

KL_WEIGHT = 16.0
EPSILON = 1e-05


def passed_along(array, axis, by):
    devices = lax.axis_size(axis)
    pairs = [(i, i + by) for i in range(devices) if 0 <= i + by < devices]
    return lax.ppermute(array, axis, pairs)


LATENTS_PER_ROW = 4
LANES = 128
PAIR_BLOCK = 2048
CONVERT_ROWS = 256
UNROLL = 32
INNER = 2


def gather_kernel(idx_ref, block_ref, out_ref, table, picked):
    step = pl.program_id(1)
    rows = block_ref.shape[0]

    @pl.when(step < LATENTS_PER_ROW)
    def _():
        def convert(i, carry):
            at = pl.multiple_of(i * CONVERT_ROWS, CONVERT_ROWS)
            table[pl.ds(step * rows + at, CONVERT_ROWS), :] = block_ref[
                pl.ds(at, CONVERT_ROWS), :
            ].astype(jnp.float32)
            return carry

        lax.fori_loop(0, rows // CONVERT_ROWS, convert, 0)

    @pl.when(step >= LATENTS_PER_ROW)
    def _():
        first = (step - LATENTS_PER_ROW) * PAIR_BLOCK

        def pick(i, carry):
            at = pl.multiple_of(i * UNROLL, UNROLL)
            loaded = [table[pl.ds(idx_ref[first + at + k], 1), :] for k in range(UNROLL)]
            for k in range(UNROLL):
                picked[pl.ds(at + k, 1), :] = loaded[k]
            return carry

        lax.fori_loop(0, PAIR_BLOCK // UNROLL, pick, 0)
        out_ref[...] = picked[...].astype(out_ref.dtype)


def gather_rows(decoder, all_idx):
    rows, wide = decoder.shape
    features = wide // LATENTS_PER_ROW
    parts = features // LANES
    pairs = all_idx.size
    flat = all_idx.reshape(pairs)
    table_row = (flat % LATENTS_PER_ROW) * rows + flat // LATENTS_PER_ROW

    def in_block(part, step, idx_ref):
        loading = step < LATENTS_PER_ROW
        following = jnp.minimum(part + 1, parts - 1)
        return (0, jnp.where(loading, step * parts + part, following))

    def out_block(part, step, idx_ref):
        return (jnp.maximum(step - LATENTS_PER_ROW, 0), part)

    return pl.pallas_call(
        gather_kernel,
        out_shape=jax.ShapeDtypeStruct((pairs, features), decoder.dtype),
        grid_spec=pltpu.PrefetchScalarGridSpec(
            num_scalar_prefetch=1,
            grid=(parts, LATENTS_PER_ROW + pairs // PAIR_BLOCK),
            in_specs=[pl.BlockSpec((rows, LANES), in_block)],
            out_specs=pl.BlockSpec((PAIR_BLOCK, LANES), out_block),
            scratch_shapes=[
                pltpu.VMEM((LATENTS_PER_ROW * rows, LANES), jnp.float32),
                pltpu.VMEM((PAIR_BLOCK, LANES), jnp.float32),
            ],
        ),
        compiler_params=pltpu.CompilerParams(vmem_limit_bytes=52 * 1024 * 1024),
    )(table_row, decoder)


def decode_rows(decoder, all_idx, every_code_value, decoder_offset_bias):
    tokens, top_count = all_idx.shape
    step_rows = math.gcd(tokens, 1024)
    idx_blocks = all_idx.reshape(tokens // step_rows, step_rows, top_count)
    val_blocks = every_code_value.reshape(tokens // step_rows, step_rows, top_count)

    def decode_one_block(index_value_pair):
        decoder_weight_rows = jnp.take(decoder, index_value_pair[0], axis=0)
        return jnp.einsum(
            "bk,bkc->bc",
            index_value_pair[1],
            decoder_weight_rows,
            preferred_element_type=jnp.float32,
        )

    summed = lax.map(decode_one_block, (idx_blocks, val_blocks)).reshape(tokens, decoder.shape[1])
    return summed + decoder_offset_bias.astype(jnp.float32)[None, :]


def code_grads(decoder, all_idx, resid_grad):
    tokens, top_count = all_idx.shape
    step_rows = math.gcd(tokens, 1024)
    idx_blocks = all_idx.reshape(tokens // step_rows, step_rows, top_count)
    grad_blocks = resid_grad.reshape(tokens // step_rows, step_rows, resid_grad.shape[1])

    def code_one_block(index_gradient_pair):
        decoder_weight_rows = jnp.take(decoder, index_gradient_pair[0], axis=0)
        upper = lax.optimization_barrier(index_gradient_pair[1].astype(jnp.bfloat16))
        lower = (index_gradient_pair[1] - upper.astype(jnp.float32)).astype(jnp.bfloat16)
        first = jnp.einsum(
            "bc,bkc->bk", upper, decoder_weight_rows, preferred_element_type=jnp.float32
        )
        second_member = jnp.einsum(
            "bc,bkc->bk", lower, decoder_weight_rows, preferred_element_type=jnp.float32
        )
        return first + second_member

    return lax.map(code_one_block, (idx_blocks, grad_blocks)).reshape(tokens, top_count)


def attend(query_new, query_old, keys_new, keys_old, mask_layout, first_pos, block_len):
    range_len = query_new.shape[0]
    band_blocks = mask_layout.shape[1] - 1
    score_scale = 1.0 / math.sqrt(query_new.shape[1])
    query_at = first_pos + jnp.arange(range_len, dtype=jnp.int32)
    key_at = first_pos - range_len + jnp.arange(2 * range_len, dtype=jnp.int32)
    query_block = jnp.floor_divide(query_at, block_len)
    key_block = jnp.floor_divide(key_at, block_len)
    rel_slot = key_block[None, :] - query_block[:, None] + band_blocks
    layout_rows = lax.dynamic_slice_in_dim(
        mask_layout, first_pos // block_len, range_len // block_len, 0
    )
    layout_rows = jnp.repeat(layout_rows, block_len, axis=0)
    slot_ids = jnp.arange(band_blocks + 1, dtype=jnp.int32)
    layout_bit = jnp.sum(
        jnp.where(rel_slot[:, :, None] == slot_ids[None, None, :], layout_rows[:, None, :], 0),
        axis=2,
    )
    visible = (layout_bit > 0) & (key_block[None, :] >= 0) & (key_at[None, :] <= query_at[:, None])

    def softmax_rows(query_side, key_side):
        scores = (
            jnp.einsum("qe,ke->qk", query_side, key_side, preferred_element_type=jnp.float32)
            * score_scale
        )
        scores = jnp.where(visible, scores, -jnp.inf)
        row_max = jnp.max(scores, axis=1, keepdims=True)
        exp_scores = jnp.exp(scores - row_max)
        return exp_scores / jnp.sum(exp_scores, axis=1, keepdims=True)

    new_probs = softmax_rows(query_new, keys_new)
    old_probs = softmax_rows(query_old, keys_old)
    score_grad = (KL_WEIGHT * score_scale * (new_probs - old_probs)).astype(jnp.bfloat16)
    query_grad = jnp.einsum("qk,ke->qe", score_grad, keys_new, preferred_element_type=jnp.float32)
    key_gradient = jnp.einsum(
        "qk,qe->ke", score_grad, query_new, preferred_element_type=jnp.float32
    )
    return (query_grad.astype(jnp.bfloat16), key_gradient[:range_len], key_gradient[range_len:])


def local_any(
    codes_idx,
    codes_val,
    decoder,
    decoder_offset_bias,
    norm_gain,
    w_query,
    w_key,
    orig_queries,
    orig_keys,
    mask_layout,
):
    seq_count = lax.axis_size("seq")
    seq_index = lax.axis_index("seq")
    tok_rows = codes_idx.shape[0]
    heads_here = orig_queries.shape[0]
    head_dim = orig_keys.shape[1]
    all_heads = w_query.shape[1] // head_dim
    model_width = decoder_offset_bias.shape[0] * seq_count * lax.axis_size("lat")
    ranges = seq_count // heads_here
    range_len = tok_rows * heads_here
    block_len = tok_rows * seq_count // mask_layout.shape[0]
    flat_shape = (heads_here * tok_rows, head_dim)
    all_idx, every_code_value = (
        lax.all_gather(codes_idx, "seq", axis=0, tiled=True),
        lax.all_gather(codes_val, "seq", axis=0, tiled=True),
    )
    features = decoder_offset_bias.shape[0]
    dec_local = decoder.reshape(decoder.shape[1] * LATENTS_PER_ROW, features)
    residual = decode_rows(dec_local, all_idx, every_code_value, decoder_offset_bias)
    residual = residual.astype(jnp.bfloat16)
    resid_f32 = residual.astype(jnp.float32)
    squares = lax.psum(jnp.sum(resid_f32 * resid_f32, axis=1), ("seq", "lat"))
    inv_rms = lax.rsqrt(squares / model_width + EPSILON)
    gain_f32 = norm_gain.astype(jnp.float32)
    normed = (resid_f32 * inv_rms[:, None] * gain_f32[None, :]).astype(jnp.bfloat16)
    local_rows = lax.all_to_all(normed, "seq", split_axis=0, concat_axis=1, tiled=True)
    wq_rows, wk_rows = (
        lax.all_gather(w_query, "seq", axis=0, tiled=True),
        lax.all_gather(w_key, "seq", axis=0, tiled=True),
    )
    wq_heads = wq_rows.reshape(wq_rows.shape[0], all_heads, head_dim)
    query_part = jnp.einsum("td,dhe->hte", local_rows, wq_heads, preferred_element_type=jnp.float32)
    key_part = jnp.dot(local_rows, wk_rows, preferred_element_type=jnp.float32)
    query_mine = lax.psum_scatter(query_part, "lat", scatter_dimension=0, tiled=True)
    key_full = lax.psum(key_part, "lat")
    query_send = query_mine.astype(jnp.bfloat16).reshape(flat_shape)
    old_send = orig_queries.reshape(flat_shape)
    key_many = jnp.broadcast_to(
        key_full.astype(jnp.bfloat16)[None], (heads_here, tok_rows, head_dim)
    )
    old_many = jnp.broadcast_to(orig_keys[None], (heads_here, tok_rows, head_dim))
    first_pos = seq_index % ranges * range_len
    query_new, query_old, keys_new, keys_old = (
        lax.all_to_all(query_send, "seq", split_axis=0, concat_axis=0, tiled=True),
        lax.all_to_all(old_send, "seq", split_axis=0, concat_axis=0, tiled=True),
        lax.all_to_all(
            key_many.reshape(flat_shape), "seq", split_axis=0, concat_axis=0, tiled=True
        ),
        lax.all_to_all(
            old_many.reshape(flat_shape), "seq", split_axis=0, concat_axis=0, tiled=True
        ),
    )
    prev_new, prev_old = passed_along((keys_new, keys_old), "seq", 1)
    query_grad, key_grad_prev, key_grad_own = attend(
        query_new,
        query_old,
        jnp.concatenate([prev_new, keys_new], axis=0),
        jnp.concatenate([prev_old, keys_old], axis=0),
        mask_layout,
        first_pos,
        block_len,
    )
    query_grad_wide = query_grad.astype(jnp.float32)
    key_next = passed_along(key_grad_prev.astype(jnp.bfloat16), "seq", -1).astype(
        key_grad_prev.dtype
    )
    query_back, key_back = (
        lax.all_to_all(
            query_grad_wide.astype(jnp.bfloat16), "seq", split_axis=0, concat_axis=0, tiled=True
        ).astype(query_grad_wide.dtype),
        lax.all_to_all(
            (key_grad_own + key_next).astype(jnp.bfloat16),
            "seq",
            split_axis=0,
            concat_axis=0,
            tiled=True,
        ).astype(jnp.float32),
    )
    key_local = jnp.sum(key_back.reshape(heads_here, tok_rows, head_dim), axis=0)
    key_total = lax.psum(key_local.astype(jnp.bfloat16), "lat")
    query_heads_grad = query_back.astype(jnp.bfloat16).reshape(heads_here, tok_rows, head_dim)
    query_all = lax.all_gather(query_heads_grad, "lat", axis=0, tiled=True)
    normed_grad = jnp.einsum("hte,dhe->td", query_all, wq_heads, preferred_element_type=jnp.float32)
    normed_grad = normed_grad + jnp.einsum(
        "te,de->td", key_total, wk_rows, preferred_element_type=jnp.float32
    )
    normed_grad = normed_grad.astype(jnp.bfloat16)
    grad_cols = lax.all_to_all(normed_grad, "seq", split_axis=1, concat_axis=0, tiled=True).astype(
        jnp.float32
    )
    inner_sum = lax.psum(jnp.sum(grad_cols * gain_f32[None, :] * resid_f32, axis=1), ("seq", "lat"))
    resid_grad = (
        gain_f32[None, :] * inv_rms[:, None] * grad_cols
        - resid_f32 * (inv_rms * inv_rms * inv_rms * inner_sum / model_width)[:, None]
    )
    grad_part = code_grads(dec_local, all_idx, resid_grad)
    grad_seq = lax.psum_scatter(grad_part, "seq", scatter_dimension=0, tiled=True)
    return lax.psum(grad_seq, "lat")


def exchange_kernel(axes, lanes_of, count, kinds, *refs):
    sources, results = refs[:count], refs[count : 2 * count]
    send_sem, recv_sem, local_sem = refs[2 * count :]
    peers = math.prod(lanes_of)
    seq_index = lax.axis_index("seq")
    if axes[0] == "seq_outer":
        me = seq_index // INNER
    elif axes[0] == "seq_inner":
        me = lax.rem(seq_index, INNER)
    else:
        me = lax.axis_index(axes[0])
    if len(axes) > 1:
        me = me * lanes_of[1] + lax.axis_index(axes[1])

    def device(peer):
        if axes[0] == "seq_outer":
            return {"seq": peer * INNER + lax.rem(seq_index, INNER)}
        if axes[0] == "seq_inner":
            return {"seq": seq_index // INNER * INNER + peer}
        if len(axes) > 1:
            return {axes[0]: peer // lanes_of[1], axes[1]: lax.rem(peer, lanes_of[1])}
        return {axes[0]: peer}

    def source(a, peer):
        if kinds[a] == "gather":
            return sources[a]
        return sources[a].at[peer // (peers // sources[a].shape[0])]

    barrier = pltpu.get_barrier_semaphore()
    for d in range(1, peers):
        pl.semaphore_signal(
            barrier,
            inc=1,
            device_id=device(lax.rem(me + d, peers)),
            device_id_type=pl.DeviceIdType.MESH,
        )
    own = [
        pltpu.make_async_copy(source(a, me), results[a].at[me], local_sem.at[a])
        for a in range(count)
    ]
    for copy in own:
        copy.start()
    pl.semaphore_wait(barrier, peers - 1)

    def remote(a, d, slot):
        peer = lax.rem(me + d, peers)
        return pltpu.make_async_remote_copy(
            src_ref=source(a, peer),
            dst_ref=results[a].at[slot],
            send_sem=send_sem.at[a, d],
            recv_sem=recv_sem.at[a, d],
            device_id=device(peer),
            device_id_type=pl.DeviceIdType.MESH,
        )

    for a in range(count):
        for d in range(1, peers):
            remote(a, d, me).start()
    for copy in own:
        copy.wait()
    for a in range(count):
        for d in range(1, peers):
            remote(a, d, lax.rem(me + peers - d, peers)).wait_recv()
    for a in range(count):
        for d in range(1, peers):
            remote(a, d, me).wait_send()


def exchange(axes, collective_id, *items):
    kinds = [kind for kind, _ in items]
    arrays = [array for _, array in items]
    extent = {"seq_inner": INNER, "seq_outer": lax.axis_size("seq") // INNER}
    sizes = [extent[axis] if axis in extent else lax.axis_size(axis) for axis in axes]
    peers = math.prod(sizes)
    shapes = [
        jax.ShapeDtypeStruct((peers,) + (a.shape if kind == "gather" else a.shape[1:]), a.dtype)
        for kind, a in items
    ]
    count = len(items)
    return pl.pallas_call(
        functools.partial(exchange_kernel, axes, sizes, count, kinds),
        out_shape=shapes,
        in_specs=[pl.BlockSpec(memory_space=pltpu.VMEM)] * count,
        out_specs=[pl.BlockSpec(memory_space=pltpu.VMEM)] * count,
        scratch_shapes=[
            pltpu.SemaphoreType.DMA((count, peers)),
            pltpu.SemaphoreType.DMA((count, peers)),
            pltpu.SemaphoreType.DMA((count,)),
        ],
        compiler_params=pltpu.CompilerParams(
            collective_id=collective_id,
            has_side_effects=True,
            vmem_limit_bytes=32 * 1024 * 1024,
        ),
    )(*arrays)


def as_tile(vectors):
    missing = LANES - vectors.shape[-1]
    padded = jnp.pad(vectors, [(0, 0)] * (vectors.ndim - 1) + [(0, missing)])
    return jnp.broadcast_to(padded[..., None, :], padded.shape[:-1] + (8, LANES))


def local(
    codes_idx,
    codes_val,
    decoder,
    decoder_offset_bias,
    norm_gain,
    w_query,
    w_key,
    orig_queries,
    orig_keys,
    mask_layout,
):
    seq_count, lat_count = lax.axis_size("seq"), lax.axis_size("lat")
    features = decoder_offset_bias.shape[0]
    heads_here = orig_queries.shape[0]
    tok_rows, top_count = codes_idx.shape
    ranges = seq_count // heads_here
    if features % LANES or ranges != lat_count or seq_count % INNER:
        return local_any(
            codes_idx,
            codes_val,
            decoder,
            decoder_offset_bias,
            norm_gain,
            w_query,
            w_key,
            orig_queries,
            orig_keys,
            mask_layout,
        )
    peers = seq_count * lat_count
    head_dim = orig_keys.shape[1]
    all_heads = heads_here * lat_count
    model_width = features * peers
    tokens = tok_rows * seq_count
    range_len = tokens // ranges
    sub = tok_rows // ranges
    block_len = tokens // mask_layout.shape[0]
    this_range = lax.axis_index("seq") % ranges
    both = ("seq", "lat")

    def by_position(array, sub=sub):
        cut = array.reshape(seq_count, ranges, sub, *array.shape[1:])
        return jnp.swapaxes(cut, 0, 1).reshape(array.shape)

    def by_token(array):
        cut = array.reshape(ranges, seq_count, sub, *array.shape[1:])
        return jnp.swapaxes(cut, 0, 1).reshape(array.shape)

    flat_rows = tok_rows * top_count // LANES
    old_half = lax.dynamic_slice_in_dim(orig_keys, lax.axis_index("lat") * sub, sub, 0)
    idx_all, val_all, query_old, old_half = exchange(
        ("seq",),
        0,
        ("gather", codes_idx.reshape(flat_rows, LANES)),
        ("gather", codes_val.reshape(flat_rows, LANES)),
        ("scatter", orig_queries.reshape(seq_count, sub, head_dim)),
        ("gather", old_half),
    )
    idx_all = by_position(idx_all.reshape(seq_count * flat_rows, LANES), flat_rows // ranges)
    val_all = by_position(val_all.reshape(seq_count * flat_rows, LANES), flat_rows // ranges)
    val_all = val_all.reshape(tokens, top_count)
    query_old = query_old.reshape(range_len, head_dim)

    picked_rows = gather_rows(decoder[0], idx_all).reshape(tokens, top_count, features)
    residual = jnp.einsum("bk,bkc->bc", val_all, picked_rows, preferred_element_type=jnp.float32)
    residual = (residual + decoder_offset_bias.astype(jnp.float32)[None, :]).astype(jnp.bfloat16)
    resid_f32 = residual.astype(jnp.float32)
    gain_f32 = norm_gain.astype(jnp.float32)
    squares = jnp.sum(resid_f32 * resid_f32, axis=1)
    scaled = (resid_f32 * gain_f32[None, :]).astype(jnp.bfloat16)

    wq_heads = w_query.reshape(features, all_heads, head_dim)
    query_part = jnp.einsum("td,dhe->hte", scaled, wq_heads, preferred_element_type=jnp.float32)
    key_part = jnp.dot(scaled, w_key, preferred_element_type=jnp.float32)
    query_pair, key_pair, square_pair, keys_old = exchange(
        ("lat",),
        1,
        ("scatter", query_part.astype(jnp.bfloat16).reshape(lat_count, -1, head_dim)),
        ("scatter", key_part.astype(jnp.bfloat16).reshape(lat_count, range_len, head_dim)),
        ("scatter", as_tile(squares.reshape(lat_count * seq_count, sub)).reshape(lat_count, -1, LANES)),
        ("gather", old_half.reshape(range_len, head_dim)),
    )
    keys_old = keys_old.reshape(tokens, head_dim)

    def pair_sum(array):
        return jnp.sum(array.astype(jnp.float32), axis=0).astype(array.dtype)

    outer = seq_count // INNER

    def inner_first(array, *shape):
        cut = array.reshape(outer, INNER, *shape)
        return jnp.swapaxes(cut, 0, 1).reshape(INNER, -1, shape[-1])

    query_parts, key_parts, square_parts = exchange(
        ("seq_inner",),
        6,
        ("scatter", inner_first(pair_sum(query_pair), range_len, head_dim)),
        ("scatter", inner_first(pair_sum(key_pair), sub, head_dim)),
        ("scatter", inner_first(pair_sum(square_pair), 8, LANES)),
    )
    query_parts, key_parts, square_parts = exchange(
        ("seq_outer",),
        8,
        ("scatter", pair_sum(query_parts).reshape(outer, range_len, head_dim)),
        ("scatter", pair_sum(key_parts).reshape(outer, sub, head_dim)),
        ("scatter", pair_sum(square_parts).reshape(outer, 8, LANES)),
    )
    query_raw = jnp.sum(query_parts.astype(jnp.float32), axis=0)
    key_raw = jnp.sum(key_parts.astype(jnp.float32), axis=0)
    inv_here = lax.rsqrt(jnp.sum(square_parts[:, 0, :sub], axis=0) / model_width + EPSILON)
    key_here = (key_raw * inv_here[:, None]).astype(jnp.bfloat16)
    keys_new, inv_tiles = exchange(both, 2, ("gather", key_here), ("gather", as_tile(inv_here)))
    keys_new = by_position(keys_new.reshape(tokens, head_dim))
    inv_rms = by_position(inv_tiles[:, 0, :sub].reshape(tokens))
    first_pos = this_range * range_len
    inv_range = lax.dynamic_slice_in_dim(inv_rms, first_pos, range_len, 0)
    query_new = (query_raw * inv_range[:, None]).astype(jnp.bfloat16)

    def window(keys):
        padded = jnp.pad(keys, ((range_len, 0), (0, 0)))
        return lax.dynamic_slice_in_dim(padded, first_pos, 2 * range_len, 0)

    query_grad, key_grad_prev, key_grad_own = attend(
        query_new,
        query_old,
        window(keys_new),
        window(keys_old),
        mask_layout,
        first_pos,
        block_len,
    )
    key_grad = lax.dynamic_update_slice_in_dim(
        jnp.zeros(((ranges + 1) * range_len, head_dim), jnp.float32),
        jnp.concatenate([key_grad_prev, key_grad_own], axis=0),
        first_pos,
        0,
    )[range_len:]
    query_inner = jnp.sum(query_grad.astype(jnp.float32) * query_new.astype(jnp.float32), axis=1)
    query_grads, key_grad_parts, inner_parts = exchange(
        ("seq_inner",),
        3,
        ("gather", query_grad),
        ("scatter", inner_first(by_token(key_grad.astype(jnp.bfloat16)), tok_rows, head_dim)),
        ("gather", query_inner.reshape(range_len // LANES, LANES)),
    )
    query_grads, key_grad_parts, inner_parts = exchange(
        ("seq_outer",),
        9,
        ("gather", query_grads.reshape(-1, head_dim)),
        ("scatter", pair_sum(key_grad_parts).reshape(outer, tok_rows, head_dim)),
        ("gather", inner_parts.reshape(-1, LANES)),
    )
    query_grads, key_grad_pair, inner_parts = exchange(
        ("lat",),
        7,
        ("gather", query_grads.reshape(-1, head_dim)),
        ("scatter", pair_sum(key_grad_parts).reshape(lat_count, sub, head_dim)),
        ("gather", inner_parts.reshape(-1, LANES)),
    )
    key_grad_here = pair_sum(key_grad_pair)
    (key_grads,) = exchange(both, 4, ("gather", key_grad_here))
    key_grads = by_position(key_grads.reshape(tokens, head_dim))

    inner = jnp.sum(inner_parts.reshape(all_heads, tokens), axis=0)
    inner = inner + jnp.sum(key_grads.astype(jnp.float32) * keys_new.astype(jnp.float32), axis=1)
    query_grads = query_grads.reshape(all_heads, tokens, head_dim)
    normed_grad = jnp.einsum("hte,dhe->td", query_grads, wq_heads, preferred_element_type=jnp.float32)
    normed_grad = normed_grad + jnp.einsum(
        "te,de->td", key_grads, w_key, preferred_element_type=jnp.float32
    )
    resid_grad = (
        gain_f32[None, :] * inv_rms[:, None] * normed_grad
        - resid_f32 * (inv_rms * inv_rms * inner / model_width)[:, None]
    ).astype(jnp.bfloat16)
    grad_part = jnp.einsum("bc,bkc->bk", resid_grad, picked_rows, preferred_element_type=jnp.float32)
    grad_part = by_token(grad_part.astype(jnp.bfloat16)).reshape(seq_count, flat_rows, LANES)
    (grad_parts,) = exchange(both, 5, ("scatter", grad_part))
    grad_parts = grad_parts.astype(jnp.float32)
    return jnp.sum(grad_parts, axis=0).reshape(tok_rows, top_count)


def solution(mesh):
    in_specs = (
        P(("grp", "seq"), None),
        P(("grp", "seq"), None),
        P(("seq", "lat"), None, None),
        P(("seq", "lat")),
        P(("seq", "lat")),
        P(("seq", "lat"), None),
        P(("seq", "lat"), None),
        P("lat", ("grp", "seq"), None),
        P(("grp", "seq"), None),
        P("grp", None),
    )
    out_specs = P(("grp", "seq"), None)
    return jax.shard_map(local, mesh=mesh, in_specs=in_specs, out_specs=out_specs, check_vma=False)
```
